128 devices in a mesh: row: 4 (over x_hi, core), col: 8 (over y, x_lo), day: 4 (over z).
Axes of the slice: x: 4 (x_hi: 2, x_lo: 2; x = x_hi * 2 + x_lo), y: 4, z: 4, core: 2. Of those that a mesh axis runs over, the one named last changes fastest.
Arguments:
- spectra: bfloat16 [64, 2, 512, 256], P('day', None, ('col', 'row')), may hold values from -12 to 12
- validity: int32 [64, 512], P('day', ('col', 'row')), may hold values from 0 to 1, as said below
Outputs:
- correlations: float32 [512, 512, 512], P('row', 'col', 'day')
The draws below stay inside these ranges and needn't reach their ends.
Inputs may be any that keep to these rules, and one draw needn't show every extreme that they name: `validity`: 1 marks a usable window of a channel; each channel has its own share of usable windows, and some channels have none.
All inputs are finite; a program needn't handle non-finite values.
Results may differ from the reference program's by a relative error of at most 0.0003.
Values may be sent and summed in bfloat16 or wider, within the bound.
A program may use at most 128 MiB of HBM per device.

```python
import math
import jax
import jax.numpy as jnp
from jax import lax

F = 256
LAGS = 512
CH = 512
WINDOWS = 64


def draw_validity(key, part):
    key = jax.random.fold_in(key, 7)
    level_key, roll_key = jax.random.split(key)
    levels = jax.random.randint(level_key, (1, CH), 0, 9)
    rolls = jax.random.randint(roll_key, (WINDOWS, CH), 0, 8)
    return (rolls < levels).astype(jnp.int32)


def block_scale(rng, dims, cuts, least, largest):
    gain = 1.0
    for axis_at, parts in cuts:
        steps = jax.random.uniform(jax.random.fold_in(jax.random.fold_in(rng, 6), axis_at), (parts,), jnp.float32, least / len(cuts), largest / len(cuts))
        gain = gain * jnp.repeat(jnp.exp(steps), dims[axis_at] // parts).reshape((-1,) + (1,) * (len(dims) - 1 - axis_at))
    return gain


def gaussian(own_key, extent, width, most, cuts=(), kind=jnp.bfloat16):
    loudness = block_scale(own_key, extent, cuts, -0.22, 0.18) if cuts else 1.0
    values = jax.random.normal(own_key, extent, jnp.float32) * width * loudness
    return jnp.minimum(jnp.maximum(values, -most), most).astype(kind)


def setup_inputs(seed: int = 0) -> dict:
    arg_keys = jax.random.split(jax.random.key(seed), 3)
    return {
        "spectra": gaussian(arg_keys[0], (WINDOWS, 2, CH, F), 2.0, 12.0, ((0, 4), (2, 32))),
        "validity": draw_validity(jax.random.fold_in(arg_keys[2], 71), 0),
    }


def lag_table():
    lag_index = jnp.arange(LAGS, dtype=jnp.int32) - LAGS // 2
    freq_index = jnp.arange(F, dtype=jnp.int32)
    product_mod = jnp.mod(lag_index[:, None] * freq_index[None, :], 2 * F)
    phases = 2.0 * math.pi / (2 * F) * product_mod.astype(jnp.float32)
    return jnp.stack([jnp.cos(phases), -jnp.sin(phases)]) / math.sqrt(F)

def reference(spectra, validity):
    valid_mask = validity.astype(jnp.float32)
    cleaned = spectra.astype(jnp.float32) * valid_mask[:, None, :, None]
    swapped = jnp.stack([cleaned[:, 1], -cleaned[:, 0]], axis=1)
    left_side = jnp.stack([cleaned, swapped])
    stacked = jnp.einsum('swcif,wcjf->sijf', left_side, cleaned, precision=lax.Precision.HIGHEST)
    pair_count = jnp.dot(valid_mask.T, valid_mask, precision=lax.Precision.HIGHEST)
    numerator = jnp.einsum('stf,sijf->ijt', lag_table(), stacked, precision=lax.Precision.HIGHEST)
    return numerator / jnp.maximum(pair_count, 1.0)[:, :, None]
```

```python
import math

import jax
import jax.numpy as jnp
import ml_dtypes
import numpy as np
from jax import lax
from jax.experimental import pallas as pl
from jax.experimental.pallas import tpu as pltpu
from jax.sharding import PartitionSpec as P

F = 256
LAGS = 512
ROWS, COLS, DAYS = 4, 8, 4
PACK = 4
GROUPS = F // PACK
SLOTS = GROUPS + 1
WIDE = 128
CHUNKS = [(0, 9)] + [(1 + 8 * k, 8) for k in range(1, 8)]
ORDER = (0, 2, 1, 3)
MESH = pl.DeviceIdType.MESH
NT = (((1,), (1,)), ((), ()))


def lag_tables():
    lag = np.arange(LAGS) - LAGS // 2
    freq = np.arange(F)
    phase = 2.0 * math.pi / (2 * F) * np.mod(lag[:, None] * freq[None, :], 2 * F)
    both = np.stack([np.cos(phase), -np.sin(phase)]) / math.sqrt(F)
    both = both.reshape(2, DAYS, LAGS // DAYS, PACK, GROUPS).transpose(1, 2, 4, 3, 0)
    both = both.reshape(DAYS, LAGS // DAYS, 2 * F).astype(np.float32)
    high = both.astype(ml_dtypes.bfloat16)
    low = (both - high.astype(np.float32)).astype(ml_dtypes.bfloat16)
    return np.concatenate([high, low], axis=1)


def own_unit(spectra, validity):
    windows, _, channels, _ = spectra.shape
    flags = validity.astype(jnp.bfloat16)
    cleaned = spectra * flags[:, None, :, None]
    split = cleaned.reshape(windows, 2, channels, PACK, GROUPS)
    packed = jnp.transpose(split, (4, 2, 3, 1, 0)).reshape(GROUPS, channels, WIDE)
    first = jnp.pad(flags.T, ((0, 0), (0, WIDE - windows)))
    return jnp.concatenate([first[None], packed])


def gather_kernel(unit, near, full, recv, sent, here):
    row, col, day = lax.axis_index("row"), lax.axis_index("col"), lax.axis_index("day")
    core, x_lo, y = row % 2, col % 2, col // 2
    sibling = {"row": row + 1 - 2 * core}
    opposite = {"row": (row + 2) % ROWS}
    partner = {"col": col + 1 - 2 * x_lo}
    up_y, down_y = {"col": (col + 2) % COLS}, {"col": (col + COLS - 2) % COLS}
    up, down = {"day": (day + 1) % DAYS}, {"day": (day + DAYS - 1) % DAYS}
    day_up, day_down, day_far = (day + 1) % DAYS, (day + DAYS - 1) % DAYS, (day + 2) % DAYS
    others = (day_down, day_up, day_far)
    offset = (y + 4 - row) % 4
    home = offset == 0
    relay_up = jnp.logical_and(core == 1, offset == 1)
    relay_down = jnp.logical_and(core == 0, offset == 3)
    far = offset == 2
    mine = pl.ds(2 * core, 2)
    theirs = pl.ds(2 - 2 * core, 2)

    barrier = pltpu.get_barrier_semaphore()
    for peer in (sibling, opposite, partner, up_y, down_y, up, down):
        pl.semaphore_signal(barrier, inc=1, device_id=peer, device_id_type=MESH)
    pl.semaphore_wait(barrier, 7)

    pending = []

    def send(k, src, dst, slot, send_slot, peer, when=None):
        def make():
            return pltpu.make_async_remote_copy(
                src_ref=src, dst_ref=dst, send_sem=sent.at[k, send_slot], recv_sem=recv.at[k, slot],
                device_id=peer, device_id_type=MESH)
        if when is None:
            make().start()
        else:
            pl.when(when)(lambda: make().start())
        pending.append((make, when))

    def arrive(k, dst, slot, when=None):
        def wait():
            pltpu.make_async_copy(dst, dst, recv.at[k, slot]).wait()
        if when is None:
            wait()
        else:
            pl.when(when)(wait)

    def span(k):
        return pl.ds(*CHUNKS[k])

    def c_at(k, d, part):
        return near.at[d, span(k), part]

    def r_at(k, d, side, part=pl.ds(0, 4)):
        return full.at[d, span(k), side, part]

    def local(src, dst, k, slot):
        copy = pltpu.make_async_copy(src, dst, here.at[k, slot])
        copy.start()
        return copy

    my_unit = 2 * core + row // 2
    both = pl.ds(0, 2)

    def start_units(k):
        place = near.at[day, span(k), my_unit]
        send(k, unit.at[span(k)], place, 0, 0, opposite)
        local(unit.at[span(k)], place, k, 0).wait()

    def spread_units(k):
        other = 2 * core + 1 - row // 2
        arrive(k, near.at[day, span(k), other], 0)
        send(k, c_at(k, day, mine), c_at(k, day, mine), 1, 1, sibling)
        send(k, c_at(k, day, mine), c_at(k, day, mine), 2, 2, up)
        send(k, c_at(k, day, mine), c_at(k, day, mine), 3, 3, down)

    def seed(k):
        arrive(k, c_at(k, day, theirs), 1)
        everything = near.at[day, span(k)]
        if k % 2 == 0:
            send(k, everything, r_at(k, day, x_lo), 9, 9, up_y, home)
            send(k, everything, r_at(k, day, x_lo), 9, 10, down_y, home)
        else:
            send(k, everything, r_at(k, day, x_lo), 9, 9, partner, home)

        @pl.when(home)
        def _():
            local(everything, r_at(k, day, x_lo), k, 1).wait()

    def near_days(k):
        first, second = pl.ds(2 * core, 1), pl.ds(2 * core + 1, 1)
        arrive(k, c_at(k, day_down, mine), 2)
        send(k, c_at(k, day_down, first), c_at(k, day_down, first), 4, 4, up)
        send(k, c_at(k, day_down, mine), c_at(k, day_down, mine), 6, 6, sibling)
        arrive(k, c_at(k, day_up, mine), 3)
        send(k, c_at(k, day_up, second), c_at(k, day_up, second), 5, 5, down)
        send(k, c_at(k, day_up, mine), c_at(k, day_up, mine), 7, 7, sibling)

    def near_far(k):
        first, second = pl.ds(2 * core, 1), pl.ds(2 * core + 1, 1)
        arrive(k, c_at(k, day_far, first), 4)
        arrive(k, c_at(k, day_far, second), 5)
        send(k, c_at(k, day_far, mine), c_at(k, day_far, mine), 8, 8, sibling)

    def along_day_start(k):
        if k % 2 == 0:
            away = jnp.logical_not(home)
            block = r_at(k, day, x_lo)
            arrive(k, block, 9, away)
            send(k, block, block, 9, 9, up_y, relay_up)
            send(k, block, block, 9, 9, down_y, relay_down)
            send(k, block, block, 10, 11, up)
            send(k, block, block, 11, 12, down)
        else:
            arrive(k, r_at(k, day, 1 - x_lo), 9, home)
            block = r_at(k, day, both)
            send(k, block, block, 10, 11, up, home)
            send(k, block, block, 11, 12, down, home)
            across_y(k, day, 14)

    def across_y(k, d, slot):
        block = r_at(k, d, both)
        send(k, block, block, slot, 2 * slot - 13, up_y, home)
        send(k, block, block, slot, 2 * slot - 12, down_y, home)

    def along_day_near(k):
        if k % 2 == 0:
            block = r_at(k, day, x_lo)
            send(k, block, block, 14, 15, partner)
            part = r_at(k, day_down, x_lo, pl.ds(0, 2))
            arrive(k, r_at(k, day_down, x_lo), 10)
            send(k, part, part, 12, 13, up)
            block = r_at(k, day_down, x_lo)
            send(k, block, block, 15, 16, partner)
            part = r_at(k, day_up, x_lo, pl.ds(2, 2))
            arrive(k, r_at(k, day_up, x_lo), 11)
            send(k, part, part, 13, 14, down)
            block = r_at(k, day_up, x_lo)
            send(k, block, block, 16, 17, partner)
        else:
            part = r_at(k, day_down, 0)
            arrive(k, r_at(k, day_down, both), 10, home)
            send(k, part, part, 12, 13, up, home)
            across_y(k, day_down, 15)
            part = r_at(k, day_up, 1)
            arrive(k, r_at(k, day_up, both), 11, home)
            send(k, part, part, 13, 14, down, home)
            across_y(k, day_up, 16)

    def along_day_far(k):
        if k % 2 == 0:
            arrive(k, r_at(k, day_far, x_lo, pl.ds(0, 2)), 12)
            arrive(k, r_at(k, day_far, x_lo, pl.ds(2, 2)), 13)
            block = r_at(k, day_far, x_lo)
            send(k, block, block, 17, 18, partner)
        else:
            arrive(k, r_at(k, day_far, 0), 12, home)
            arrive(k, r_at(k, day_far, 1), 13, home)
            across_y(k, day_far, 17)

    def relay(k, slots):
        if k % 2 == 1:
            for d, slot in zip((day,) + others, range(14, 18)):
                if slot in slots:
                    block = r_at(k, d, both)
                    near_y = jnp.logical_or(offset == 1, offset == 3)
                    arrive(k, block, slot, near_y)
                    send(k, block, block, slot, 2 * slot - 13, up_y, relay_up)
                    send(k, block, block, slot, 2 * slot - 13, down_y, relay_down)

    def finish(k):
        for d, slot in zip(others, (6, 7, 8)):
            arrive(k, c_at(k, d, theirs), slot)
        for d, slot in zip((day,) + others, range(14, 18)):
            if k % 2 == 0:
                arrive(k, r_at(k, d, 1 - x_lo), slot)
            else:
                arrive(k, r_at(k, d, both), slot, far)

    count = len(CHUNKS)
    for k in range(count):
        start_units(k)
    stages = (
        spread_units,
        seed,
        near_days,
        along_day_start,
        along_day_near,
        near_far,
        along_day_far,
        lambda k: relay(k, range(14, 18)),
        finish,
    )
    for step in range(count + len(stages) - 1):
        for at in reversed(range(len(stages))):
            if 0 <= step - at < count:
                stages[at](step - at)
    for make, when in pending:
        if when is None:
            make().wait_send()
        else:
            pl.when(when)(lambda make=make: make().wait_send())


def gather(unit):
    count = len(CHUNKS)
    channels = unit.shape[1]
    return pl.pallas_call(
        gather_kernel,
        out_shape=(
            jax.ShapeDtypeStruct((DAYS, SLOTS, 4, channels, WIDE), unit.dtype),
            jax.ShapeDtypeStruct((DAYS, SLOTS, 2, 4, channels, WIDE), unit.dtype),
        ),
        in_specs=[pl.BlockSpec(memory_space=pl.ANY)],
        out_specs=(pl.BlockSpec(memory_space=pl.ANY),) * 2,
        scratch_shapes=[
            pltpu.SemaphoreType.DMA((count, 18)),
            pltpu.SemaphoreType.DMA((count, 23)),
            pltpu.SemaphoreType.DMA((count, 2)),
        ],
        compiler_params=pltpu.CompilerParams(collective_id=0, has_side_effects=True),
        name="gather_units",
    )(unit)


def swap8(block):
    return jnp.swapaxes(block, 0, 1)


def correlate_kernel(near, full, table, out, stack, inverse):
    lane = lax.broadcasted_iota(jnp.int32, (64, 2 * WIDE), 1)
    real = (lane // 16) % 2 == 0
    place = (lane // 32) % PACK

    def columns(d, slot):
        return jnp.concatenate([near[d, slot, v] for v in ORDER], axis=0)

    def rows(d, slot):
        return jnp.concatenate([full[d, slot, side, v] for side in range(2) for v in ORDER], axis=0)

    count = jnp.zeros((64, WIDE), jnp.float32)
    for d in range(DAYS):
        count += lax.dot_general(columns(d, 0), rows(d, 0), NT, preferred_element_type=jnp.float32)
    inverse[...] = 1.0 / jnp.maximum(count, 1.0)

    def stack_group(group, _):
        slot = group + 1
        total = None
        for pair in range(DAYS // 2):
            col = jnp.concatenate([columns(2 * pair, slot), columns(2 * pair + 1, slot)], axis=1).astype(jnp.float32)
            row = jnp.concatenate([rows(2 * pair, slot), rows(2 * pair + 1, slot)], axis=1)
            swapped = jnp.where(real, -pltpu.roll(col, 2 * WIDE - 16, 1), pltpu.roll(col, 16, 1))
            parts = []
            for at in range(PACK):
                for side in (col, swapped):
                    parts.append(jnp.where(place == at, side, 0.0).astype(jnp.bfloat16))
            left = jnp.concatenate(parts, axis=0)
            term = lax.dot_general(left, row, NT, preferred_element_type=jnp.float32)
            total = term if total is None else total + term
        total = total.reshape(8, 64, WIDE)
        start = pl.multiple_of(group * 8, 8)
        for at in range(0, 64, 8):
            stack[at : at + 8, pl.ds(start, 8), :] = swap8(total[:, at : at + 8, :])
        return 0

    lax.fori_loop(0, GROUPS, stack_group, 0)

    def lag_group(group, _):
        done = []
        for at in range(8):
            j = group * 8 + at
            values = stack[j]
            high = values.astype(jnp.bfloat16)
            low = (values - high.astype(jnp.float32)).astype(jnp.bfloat16)
            first = jnp.dot(table[...], high, preferred_element_type=jnp.float32)
            second = jnp.dot(table[:WIDE], low, preferred_element_type=jnp.float32)
            lags = (first[:WIDE] + first[WIDE:] + second) * inverse[pl.ds(j, 1), :]
            done.append(lags.T)
        start = pl.multiple_of(group * 8, 8)
        for at in range(0, WIDE, 8):
            out[at : at + 8, pl.ds(start, 8), :] = swap8(jnp.stack([d[at : at + 8] for d in done]))
        return 0

    lax.fori_loop(0, 8, lag_group, 0)


def correlate(near, full, table):
    return pl.pallas_call(
        correlate_kernel,
        out_shape=jax.ShapeDtypeStruct((WIDE, 64, WIDE), jnp.float32),
        in_specs=[pl.BlockSpec(memory_space=pltpu.VMEM)] * 3,
        out_specs=pl.BlockSpec(memory_space=pltpu.VMEM),
        scratch_shapes=[pltpu.VMEM((64, 2 * F, WIDE), jnp.float32), pltpu.VMEM((64, WIDE), jnp.float32)],
        compiler_params=pltpu.CompilerParams(vmem_limit_bytes=56 << 20),
        name="correlate",
    )(near, full, table)


def per_device(spectra, validity):
    table = lax.dynamic_index_in_dim(jnp.asarray(lag_tables()), lax.axis_index("day"), keepdims=False)
    near, full = gather(own_unit(spectra, validity))
    return correlate(near, full, table)


def solution(mesh):
    placed = (P("day", None, ("col", "row"), None), P("day", ("col", "row")))
    return jax.shard_map(
        per_device, mesh=mesh, in_specs=placed, out_specs=P("row", "col", "day"), check_vma=False
    )
```

```python
import math

import jax
import jax.numpy as jnp
import numpy as np
from jax import lax
from jax.experimental import pallas as pl
from jax.experimental.pallas import tpu as pltpu
from jax.sharding import PartitionSpec as P

F = 256
LAGS = 512
ROWS, COLS, DAYS = 4, 8, 4
PACK = 4
GROUPS = F // PACK
SLOTS = GROUPS + 1
WIDE = 128
CHUNKS = [(0, 9)] + [(1 + 8 * k, 8) for k in range(1, 8)]
ORDER = (0, 2, 1, 3)
MESH = pl.DeviceIdType.MESH
NT = (((1,), (1,)), ((), ()))


def lag_tables():
    lag = np.arange(LAGS) - LAGS // 2
    freq = np.arange(F)
    phase = 2.0 * math.pi / (2 * F) * np.mod(lag[:, None] * freq[None, :], 2 * F)
    both = np.stack([np.cos(phase), -np.sin(phase)]) / math.sqrt(F)
    both = both.reshape(2, DAYS, LAGS // DAYS, PACK, GROUPS).transpose(1, 2, 4, 3, 0)
    return both.reshape(DAYS, LAGS // DAYS, 2 * F).astype(np.float32)


def own_unit(spectra, validity):
    windows, _, channels, _ = spectra.shape
    flags = validity.astype(jnp.bfloat16)
    cleaned = spectra * flags[:, None, :, None]
    split = cleaned.reshape(windows, 2, channels, PACK, GROUPS)
    packed = jnp.transpose(split, (4, 2, 3, 1, 0)).reshape(GROUPS, channels, WIDE)
    first = jnp.pad(flags.T, ((0, 0), (0, WIDE - windows)))
    return jnp.concatenate([first[None], packed])


def swap8(block):
    return jnp.swapaxes(block, 0, 1)


def correlate_kernel(unit, tables, out, near, full, stack, partial, exact, table, inverse, recv, sent, here, table_sem):
    row, col, day = lax.axis_index("row"), lax.axis_index("col"), lax.axis_index("day")
    core, x_lo, y = row % 2, col % 2, col // 2
    sibling = {"row": row + 1 - 2 * core}
    opposite = {"row": (row + 2) % ROWS}
    partner = {"col": col + 1 - 2 * x_lo}
    up_y, down_y = {"col": (col + 2) % COLS}, {"col": (col + COLS - 2) % COLS}
    up, down = {"day": (day + 1) % DAYS}, {"day": (day + DAYS - 1) % DAYS}
    day_up, day_down, day_far = (day + 1) % DAYS, (day + DAYS - 1) % DAYS, (day + 2) % DAYS
    others = (day_down, day_up, day_far)
    offset = (y + 4 - row) % 4
    home = offset == 0
    relay_up = jnp.logical_and(core == 1, offset == 1)
    relay_down = jnp.logical_and(core == 0, offset == 3)
    far = offset == 2
    mine = pl.ds(2 * core, 2)
    theirs = pl.ds(2 - 2 * core, 2)

    table_copy = pltpu.make_async_copy(tables.at[day], exact, table_sem)
    table_copy.start()

    barrier = pltpu.get_barrier_semaphore()
    for peer in (sibling, opposite, partner, up_y, down_y, up, down):
        pl.semaphore_signal(barrier, inc=1, device_id=peer, device_id_type=MESH)
    pl.semaphore_wait(barrier, 7)

    pending = []

    def send(k, src, dst, slot, send_slot, peer, when=None):
        def make():
            return pltpu.make_async_remote_copy(
                src_ref=src, dst_ref=dst, send_sem=sent.at[k, send_slot], recv_sem=recv.at[k, slot],
                device_id=peer, device_id_type=MESH)
        if when is None:
            make().start()
        else:
            pl.when(when)(lambda: make().start())
        pending.append((make, when))

    def arrive(k, dst, slot, when=None):
        def wait():
            pltpu.make_async_copy(dst, dst, recv.at[k, slot]).wait()
        if when is None:
            wait()
        else:
            pl.when(when)(wait)

    def span(k):
        return pl.ds(*CHUNKS[k])

    def c_at(k, d, part):
        return near.at[d, span(k), part]

    def r_at(k, d, side, part=pl.ds(0, 4)):
        return full.at[d, span(k), side, part]

    def local(src, dst, k, slot):
        copy = pltpu.make_async_copy(src, dst, here.at[k, slot])
        copy.start()
        return copy

    my_unit = 2 * core + row // 2
    both = pl.ds(0, 2)

    def start_units(k):
        place = near.at[day, span(k), my_unit]
        send(k, unit.at[span(k)], place, 0, 0, opposite)
        local(unit.at[span(k)], place, k, 0).wait()

    def spread_units(k):
        other = 2 * core + 1 - row // 2
        arrive(k, near.at[day, span(k), other], 0)
        send(k, c_at(k, day, mine), c_at(k, day, mine), 1, 1, sibling)
        send(k, c_at(k, day, mine), c_at(k, day, mine), 2, 2, up)
        send(k, c_at(k, day, mine), c_at(k, day, mine), 3, 3, down)

    def seed(k):
        arrive(k, c_at(k, day, theirs), 1)
        everything = near.at[day, span(k)]
        if k % 2 == 0:
            send(k, everything, r_at(k, day, x_lo), 9, 9, up_y, home)
            send(k, everything, r_at(k, day, x_lo), 9, 10, down_y, home)
        else:
            send(k, everything, r_at(k, day, x_lo), 9, 9, partner, home)

        @pl.when(home)
        def _():
            local(everything, r_at(k, day, x_lo), k, 1).wait()

    def near_days(k):
        first, second = pl.ds(2 * core, 1), pl.ds(2 * core + 1, 1)
        arrive(k, c_at(k, day_down, mine), 2)
        send(k, c_at(k, day_down, first), c_at(k, day_down, first), 4, 4, up)
        send(k, c_at(k, day_down, mine), c_at(k, day_down, mine), 6, 6, sibling)
        arrive(k, c_at(k, day_up, mine), 3)
        send(k, c_at(k, day_up, second), c_at(k, day_up, second), 5, 5, down)
        send(k, c_at(k, day_up, mine), c_at(k, day_up, mine), 7, 7, sibling)

    def near_far(k):
        first, second = pl.ds(2 * core, 1), pl.ds(2 * core + 1, 1)
        arrive(k, c_at(k, day_far, first), 4)
        arrive(k, c_at(k, day_far, second), 5)
        send(k, c_at(k, day_far, mine), c_at(k, day_far, mine), 8, 8, sibling)

    def along_day_start(k):
        if k % 2 == 0:
            away = jnp.logical_not(home)
            block = r_at(k, day, x_lo)
            arrive(k, block, 9, away)
            send(k, block, block, 9, 9, up_y, relay_up)
            send(k, block, block, 9, 9, down_y, relay_down)
            send(k, block, block, 10, 11, up)
            send(k, block, block, 11, 12, down)
        else:
            arrive(k, r_at(k, day, 1 - x_lo), 9, home)
            block = r_at(k, day, both)
            send(k, block, block, 10, 11, up, home)
            send(k, block, block, 11, 12, down, home)
            across_y(k, day, 14)

    def across_y(k, d, slot):
        block = r_at(k, d, both)
        send(k, block, block, slot, 2 * slot - 13, up_y, home)
        send(k, block, block, slot, 2 * slot - 12, down_y, home)

    def along_day_near(k):
        if k % 2 == 0:
            block = r_at(k, day, x_lo)
            send(k, block, block, 14, 15, partner)
            part = r_at(k, day_down, x_lo, pl.ds(0, 2))
            arrive(k, r_at(k, day_down, x_lo), 10)
            send(k, part, part, 12, 13, up)
            block = r_at(k, day_down, x_lo)
            send(k, block, block, 15, 16, partner)
            part = r_at(k, day_up, x_lo, pl.ds(2, 2))
            arrive(k, r_at(k, day_up, x_lo), 11)
            send(k, part, part, 13, 14, down)
            block = r_at(k, day_up, x_lo)
            send(k, block, block, 16, 17, partner)
        else:
            part = r_at(k, day_down, 0)
            arrive(k, r_at(k, day_down, both), 10, home)
            send(k, part, part, 12, 13, up, home)
            across_y(k, day_down, 15)
            part = r_at(k, day_up, 1)
            arrive(k, r_at(k, day_up, both), 11, home)
            send(k, part, part, 13, 14, down, home)
            across_y(k, day_up, 16)

    def along_day_far(k):
        if k % 2 == 0:
            arrive(k, r_at(k, day_far, x_lo, pl.ds(0, 2)), 12)
            arrive(k, r_at(k, day_far, x_lo, pl.ds(2, 2)), 13)
            block = r_at(k, day_far, x_lo)
            send(k, block, block, 17, 18, partner)
        else:
            arrive(k, r_at(k, day_far, 0), 12, home)
            arrive(k, r_at(k, day_far, 1), 13, home)
            across_y(k, day_far, 17)

    def relay(k, slots):
        if k % 2 == 1:
            for d, slot in zip((day,) + others, range(14, 18)):
                if slot in slots:
                    block = r_at(k, d, both)
                    near_y = jnp.logical_or(offset == 1, offset == 3)
                    arrive(k, block, slot, near_y)
                    send(k, block, block, slot, 2 * slot - 13, up_y, relay_up)
                    send(k, block, block, slot, 2 * slot - 13, down_y, relay_down)

    def finish(k):
        for d, slot in zip(others, (6, 7, 8)):
            arrive(k, c_at(k, d, theirs), slot)
        for d, slot in zip((day,) + others, range(14, 18)):
            if k % 2 == 0:
                arrive(k, r_at(k, d, 1 - x_lo), slot)
            else:
                arrive(k, r_at(k, d, both), slot, far)

    lane = lax.broadcasted_iota(jnp.int32, (64, 2 * WIDE), 1)
    real = (lane // 16) % 2 == 0
    place = (lane // 32) % PACK

    def columns(d, slot):
        return jnp.concatenate([near[d, slot, v] for v in ORDER], axis=0)

    def rows(d, slot):
        return jnp.concatenate([full[d, slot, side, v] for side in range(2) for v in ORDER], axis=0)

    def pair_counts():
        total = jnp.zeros((64, WIDE), jnp.float32)
        for d in range(DAYS):
            total += lax.dot_general(columns(d, 0), rows(d, 0), NT, preferred_element_type=jnp.float32)
        inverse[...] = 1.0 / jnp.maximum(total, 1.0)

    def stack_group(group):
        slot = group + 1
        total = None
        for pair in range(DAYS // 2):
            col = jnp.concatenate([columns(2 * pair, slot), columns(2 * pair + 1, slot)], axis=1).astype(jnp.float32)
            row = jnp.concatenate([rows(2 * pair, slot), rows(2 * pair + 1, slot)], axis=1)
            swapped = jnp.where(real, -pltpu.roll(col, 2 * WIDE - 16, 1), pltpu.roll(col, 16, 1))
            parts = []
            for at in range(PACK):
                for side in (col, swapped):
                    parts.append(jnp.where(place == at, side, 0.0).astype(jnp.bfloat16))
            left = jnp.concatenate(parts, axis=0)
            term = lax.dot_general(left, row, NT, preferred_element_type=jnp.float32)
            total = term if total is None else total + term
        total = total.reshape(8, 64, WIDE)
        start = pl.multiple_of(group * 8, 8)
        for at in range(0, 64, 8):
            stack[at : at + 8, pl.ds(start, 8), :] = swap8(total[:, at : at + 8, :])

    def split_table():
        table_copy.wait()
        high = exact[...].astype(jnp.bfloat16)
        table[:WIDE] = high
        table[WIDE:] = (exact[...] - high.astype(jnp.float32)).astype(jnp.bfloat16)

    def half_lags(j, half):
        span = pl.ds(half * F, F)
        values = stack[j, span, :]
        high = values.astype(jnp.bfloat16)
        low = (values - high.astype(jnp.float32)).astype(jnp.bfloat16)
        first = jnp.dot(table[:, span], high, preferred_element_type=jnp.float32)
        second = jnp.dot(table[:WIDE, span], low, preferred_element_type=jnp.float32)
        return first[:WIDE] + first[WIDE:] + second

    def first_half(group):
        for at in range(8):
            partial[group * 8 + at] = half_lags(group * 8 + at, 0)

    def second_half(group):
        done = []
        for at in range(8):
            j = group * 8 + at
            done.append(((partial[j] + half_lags(j, 1)) * inverse[pl.ds(j, 1), :]).T)
        start = pl.multiple_of(group * 8, 8)
        for at in range(0, WIDE, 8):
            out[at : at + 8, pl.ds(start, 8), :] = swap8(jnp.stack([d[at : at + 8] for d in done]))

    def repeat(body, first, times):
        def step(at, _):
            body(at)
            return 0

        lax.fori_loop(first, first + times, step, 0)

    count = len(CHUNKS)
    work = []

    def ready(k):
        if k == 0:
            work.append(pair_counts)
        for at in range(0, GROUPS // count, 2):
            work.append(lambda first=k * GROUPS // count + at: repeat(stack_group, first, 2))
        if k == count // 2 - 1:
            work.append(split_table)
            for at in range(0, 8, 2):
                work.append(lambda first=at: repeat(first_half, first, 2))

    for k in range(count):
        start_units(k)
    stages = (
        spread_units,
        seed,
        near_days,
        along_day_start,
        along_day_near,
        near_far,
        along_day_far,
        lambda k: relay(k, range(14, 18)),
        finish,
    )
    for step in range(count + len(stages) - 1):
        for at in reversed(range(len(stages))):
            if 0 <= step - at < count:
                stages[at](step - at)
                if work:
                    work.pop(0)()
        if 0 <= step + 1 - len(stages) < count:
            ready(step + 1 - len(stages))
    for item in work:
        item()
    repeat(second_half, 0, 8)
    for make, when in pending:
        if when is None:
            make().wait_send()
        else:
            pl.when(when)(lambda make=make: make().wait_send())


def correlate(unit, tables):
    count = len(CHUNKS)
    channels = unit.shape[1]
    vmem = pl.BlockSpec(memory_space=pltpu.VMEM)
    return pl.pallas_call(
        correlate_kernel,
        out_shape=jax.ShapeDtypeStruct((WIDE, 64, WIDE), jnp.float32),
        in_specs=[vmem, pl.BlockSpec(memory_space=pl.ANY)],
        out_specs=vmem,
        scratch_shapes=[
            pltpu.VMEM((DAYS, SLOTS, 4, channels, WIDE), unit.dtype),
            pltpu.VMEM((DAYS, SLOTS, 2, 4, channels, WIDE), unit.dtype),
            pltpu.VMEM((64, 2 * F, WIDE), jnp.float32),
            pltpu.VMEM((64, WIDE, WIDE), jnp.float32),
            pltpu.VMEM((WIDE, 2 * F), jnp.float32),
            pltpu.VMEM((2 * WIDE, 2 * F), jnp.bfloat16),
            pltpu.VMEM((64, WIDE), jnp.float32),
            pltpu.SemaphoreType.DMA((count, 18)),
            pltpu.SemaphoreType.DMA((count, 23)),
            pltpu.SemaphoreType.DMA((count, 2)),
            pltpu.SemaphoreType.DMA,
        ],
        compiler_params=pltpu.CompilerParams(collective_id=0, has_side_effects=True, vmem_limit_bytes=52 << 20),
        name="correlate",
    )(unit, tables)


def per_device(spectra, validity):
    return correlate(own_unit(spectra, validity), jnp.asarray(lag_tables()))


def solution(mesh):
    placed = (P("day", None, ("col", "row"), None), P("day", ("col", "row")))
    return jax.shard_map(
        per_device, mesh=mesh, in_specs=placed, out_specs=P("row", "col", "day"), check_vma=False
    )
```

```python
import math

import jax
import jax.numpy as jnp
import numpy as np
from jax import lax
from jax.experimental import pallas as pl
from jax.experimental.pallas import tpu as pltpu
from jax.sharding import PartitionSpec as P

F = 256
LAGS = 512
ROWS, COLS, DAYS = 4, 8, 4
PACK = 4
GROUPS = F // PACK
SLOTS = GROUPS + 1
WIDE = 128
SIZES = (6, 9, 8, 10, 8, 8, 8, 8)
MIDDLE = 3
ORDER = (0, 2, 1, 3)
MESH = pl.DeviceIdType.MESH
NT = (((1,), (1,)), ((), ()))


def lag_tables():
    lag = np.arange(LAGS) - LAGS // 2
    freq = np.arange(F)
    phase = 2.0 * math.pi / (2 * F) * np.mod(lag[:, None] * freq[None, :], 2 * F)
    both = np.stack([np.cos(phase), -np.sin(phase)]) / math.sqrt(F)
    both = both.reshape(2, DAYS, LAGS // DAYS, PACK, GROUPS).transpose(1, 2, 4, 3, 0)
    return both.reshape(DAYS, LAGS // DAYS, 2 * F).astype(np.float32)


def own_unit(spectra, validity):
    windows, _, channels, _ = spectra.shape
    flags = validity.astype(jnp.bfloat16)
    cleaned = spectra * flags[:, None, :, None]
    split = cleaned.reshape(windows, 2, channels, PACK, GROUPS)
    packed = jnp.transpose(split, (4, 2, 3, 1, 0)).reshape(GROUPS, channels, WIDE)
    first = jnp.pad(flags.T, ((0, 0), (0, WIDE - windows)))
    return jnp.concatenate([first[None], packed])


def swap8(block):
    return jnp.swapaxes(block, 0, 1)


def correlate_kernel(unit, tables, out, near, full, stack, partial, exact, table, inverse, recv, sent, here, table_sem):
    row, col, day = lax.axis_index("row"), lax.axis_index("col"), lax.axis_index("day")
    core, x_hi, x_lo, y = row % 2, row // 2, col % 2, col // 2
    sibling = {"row": row + 1 - 2 * core}
    opposite = {"row": (row + 2) % ROWS}
    partner = {"col": col + 1 - 2 * x_lo}
    up_y, down_y = {"col": (col + 2) % COLS}, {"col": (col + COLS - 2) % COLS}
    days = [{"day": (day + step) % DAYS} for step in range(DAYS)]
    offset = (y + 4 - row) % 4
    home = offset == 0
    away = offset != 0
    beside = jnp.logical_or(offset == 1, offset == 3)
    far = offset == 2
    relay_up = jnp.logical_and(core == 1, offset == 1)
    relay_down = jnp.logical_and(core == 0, offset == 3)
    home_chip = x_hi == y // 2
    other_chip = x_hi != y // 2
    home_sibling = jnp.logical_and(home_chip, away)

    barrier = pltpu.get_barrier_semaphore()
    for peer in (sibling, opposite, partner, up_y, down_y, *days[1:]):
        pl.semaphore_signal(barrier, inc=1, device_id=peer, device_id_type=MESH)

    table_copy = pltpu.make_async_copy(tables.at[day], exact, table_sem)
    table_copy.start()

    count = len(SIZES)
    spans = [pl.ds(sum(SIZES[:k]), SIZES[k]) for k in range(count)]
    mine, theirs = pl.ds(2 * core, 2), pl.ds(2 - 2 * core, 2)
    all_units, both, later = pl.ds(0, 4), pl.ds(0, 2), pl.ds(1, DAYS - 1)
    pending = [[] for _ in range(count)]

    def act(when, body):
        if when is None:
            body()
        else:
            pl.when(when)(body)

    def send(k, src, dst, slot, peer, when=None, extra=0):
        def make():
            return pltpu.make_async_remote_copy(
                src_ref=src, dst_ref=dst, send_sem=sent.at[k, slot + extra], recv_sem=recv.at[k, slot],
                device_id=peer, device_id_type=MESH)

        act(when, lambda: make().start())
        pending[k].append((make, when))

    def arrive(k, dst, slot, when=None):
        act(when, lambda: pltpu.make_async_copy(dst, dst, recv.at[k, slot]).wait())

    def sent_all(k):
        for make, when in pending[k]:
            act(when, lambda make=make: make().wait_send())

    def n_at(k, d, part=all_units):
        return near.at[d, spans[k], part]

    def f_at(k, d, side, part=all_units):
        return full.at[d, spans[k], side, part]

    def day_sends(k, block, place, slot, when=None):
        for step in (1, 3, 2):
            send(k, block, place(DAYS - step), slot + step - 1, days[step], when)

    def day_arrivals(k, place, slot, when=None):
        for step in (1, 3, 2):
            arrive(k, place(DAYS - step), slot + step - 1, when)

    def start_units(k):
        place = near.at[0, spans[k], 2 * core + x_hi]
        send(k, unit.at[spans[k]], place, 0, opposite)
        copy = pltpu.make_async_copy(unit.at[spans[k]], place, here.at[k, 0])
        copy.start()
        return copy

    def spread_units(k):
        arrive(k, near.at[0, spans[k], 2 * core + 1 - x_hi], 0)
        copies[k].wait()
        block = n_at(k, 0, mine)
        send(k, block, block, 1, sibling)
        day_sends(k, block, lambda d: n_at(k, d, mine), 2, other_chip)

    def first_spread(k):
        arrive(k, n_at(k, 0, theirs), 1)
        block, place = n_at(k, 0), f_at(k, 0, x_lo)

        @pl.when(home)
        def _():
            copy = pltpu.make_async_copy(block, place, here.at[k, 1])
            copy.start()
            copy.wait()

        if k % 2 == 0:
            send(k, block, place, 6, up_y, home)
            send(k, block, place, 6, down_y, home, extra=6)
        else:
            send(k, block, place, 6, partner, home)

    def own_day(k):
        if k % 2 == 0:
            block = f_at(k, 0, x_lo)
            arrive(k, block, 6, away)
            send(k, block, block, 6, up_y, relay_up)
            send(k, block, block, 6, down_y, relay_down)
            day_sends(k, block, lambda d: f_at(k, d, x_lo), 7)
            send(k, block, block, 10, partner)
        else:
            arrive(k, f_at(k, 0, 1 - x_lo), 6, home)
            block = f_at(k, 0, both)
            day_sends(k, block, lambda d: f_at(k, d, both), 7, home)
            send(k, block, block, 10, up_y, home)
            send(k, block, block, 10, down_y, home, extra=3)

    def later_days(k):
        day_arrivals(k, lambda d: n_at(k, d, mine), 2, other_chip)
        block = n_at(k, later, mine)
        send(k, block, block, 5, sibling, other_chip)
        if k % 2 == 0:
            day_arrivals(k, lambda d: f_at(k, d, x_lo), 7)
            block = f_at(k, later, x_lo)
            send(k, block, block, 11, partner)
        else:
            day_arrivals(k, lambda d: f_at(k, d, both), 7, home)
            block = f_at(k, later, both)
            send(k, block, block, 11, up_y, home)
            send(k, block, block, 11, down_y, home, extra=3)
        block, place = f_at(k, later, x_lo), n_at(k, later)
        send(k, block, place, 5, sibling, home)
        act(home, lambda: pltpu.make_async_copy(block, place, here.at[k, 0]).start())

    def relay_own(k):
        if k % 2 == 1:
            relay(k, f_at(k, 0, both), 10)

    def relay_later(k):
        if k % 2 == 1:
            relay(k, f_at(k, later, both), 11)

    def relay(k, block, slot):
        arrive(k, block, slot, beside)
        send(k, block, block, slot, up_y, relay_up)
        send(k, block, block, slot, down_y, relay_down)

    def finish(k):
        arrive(k, n_at(k, later, theirs), 5, other_chip)
        arrive(k, n_at(k, later), 5, home_sibling)
        act(home, lambda: pltpu.make_async_copy(f_at(k, later, x_lo), n_at(k, later), here.at[k, 0]).wait())
        if k % 2 == 0:
            arrive(k, f_at(k, 0, 1 - x_lo), 10)
            arrive(k, f_at(k, later, 1 - x_lo), 11)
        else:
            arrive(k, f_at(k, 0, both), 10, far)
            arrive(k, f_at(k, later, both), 11, far)

    lane = lax.broadcasted_iota(jnp.int32, (64, 2 * WIDE), 1)
    real = (lane // 16) % 2 == 0
    place = (lane // 32) % PACK

    def columns(d, slot):
        return jnp.concatenate([near[d, slot, v] for v in ORDER], axis=0)

    def rows(d, slot):
        return jnp.concatenate([full[d, slot, side, v] for side in range(2) for v in ORDER], axis=0)

    def pair_counts():
        total = jnp.zeros((64, WIDE), jnp.float32)
        for d in range(DAYS):
            total += lax.dot_general(columns(d, 0), rows(d, 0), NT, preferred_element_type=jnp.float32)
        inverse[...] = 1.0 / jnp.maximum(total, 1.0)

    def stack_group(group):
        slot = group + 1
        total = None
        for pair in range(DAYS // 2):
            col = jnp.concatenate([columns(2 * pair, slot), columns(2 * pair + 1, slot)], axis=1).astype(jnp.float32)
            row = jnp.concatenate([rows(2 * pair, slot), rows(2 * pair + 1, slot)], axis=1)
            swapped = jnp.where(real, -pltpu.roll(col, 2 * WIDE - 16, 1), pltpu.roll(col, 16, 1))
            parts = []
            for at in range(PACK):
                for side in (col, swapped):
                    parts.append(jnp.where(place == at, side, 0.0).astype(jnp.bfloat16))
            left = jnp.concatenate(parts, axis=0)
            term = lax.dot_general(left, row, NT, preferred_element_type=jnp.float32)
            total = term if total is None else total + term
        total = total.reshape(8, 64, WIDE)
        start = pl.multiple_of(group * 8, 8)
        for at in range(0, 64, 8):
            stack[at : at + 8, pl.ds(start, 8), :] = swap8(total[:, at : at + 8, :])

    def split_table():
        table_copy.wait()
        high = exact[...].astype(jnp.bfloat16)
        table[:WIDE] = high
        table[WIDE:] = (exact[...] - high.astype(jnp.float32)).astype(jnp.bfloat16)

    def half_lags(j, half):
        span = pl.ds(half * F, F)
        values = stack[j, span, :]
        high = values.astype(jnp.bfloat16)
        low = (values - high.astype(jnp.float32)).astype(jnp.bfloat16)
        first = jnp.dot(table[:, span], high, preferred_element_type=jnp.float32)
        second = jnp.dot(table[:WIDE, span], low, preferred_element_type=jnp.float32)
        return first[:WIDE] + first[WIDE:] + second

    def first_half(group):
        for at in range(8):
            partial[group * 8 + at] = half_lags(group * 8 + at, 0)

    def second_half(group):
        done = []
        for at in range(8):
            j = group * 8 + at
            done.append(((partial[j] + half_lags(j, 1)) * inverse[pl.ds(j, 1), :]).T)
        start = pl.multiple_of(group * 8, 8)
        for at in range(0, WIDE, 8):
            out[at : at + 8, pl.ds(start, 8), :] = swap8(jnp.stack([d[at : at + 8] for d in done]))

    def repeat(body, first, times):
        def step(at, _):
            body(at)
            return 0

        lax.fori_loop(first, first + times, step, 0)

    work = []

    def ready(k):
        if k == 0:
            work.append(pair_counts)
        first, last = max(sum(SIZES[:k]) - 1, 0), sum(SIZES[: k + 1]) - 1
        for at in range(first, last, 2):
            work.append(lambda at=at: repeat(stack_group, at, min(2, last - at)))
        if k == MIDDLE:
            work.append(split_table)
            for at in range(0, 8, 2):
                work.append(lambda first=at: repeat(first_half, first, 2))

    pl.semaphore_wait(barrier, 8)
    copies = [start_units(k) for k in range(count)]
    stages = (spread_units, first_spread, own_day, later_days, relay_own, relay_later, finish)
    for step in range(count + len(stages) - 1):
        for at in reversed(range(len(stages))):
            if 0 <= step - at < count:
                stages[at](step - at)
                if work:
                    work.pop(0)()
        done = step + 1 - len(stages)
        if 0 <= done < count:
            ready(done)
        if 0 < done < count:
            sent_all(done - 1)
    for item in work:
        item()
    repeat(second_half, 0, 8)
    sent_all(count - 1)


def correlate(unit, tables):
    count = len(SIZES)
    channels = unit.shape[1]
    vmem = pl.BlockSpec(memory_space=pltpu.VMEM)
    return pl.pallas_call(
        correlate_kernel,
        out_shape=pltpu.VMEM((WIDE, 64, WIDE), jnp.float32),
        in_specs=[vmem, pl.BlockSpec(memory_space=pl.ANY)],
        out_specs=vmem,
        scratch_shapes=[
            pltpu.VMEM((DAYS, SLOTS, 4, channels, WIDE), unit.dtype),
            pltpu.VMEM((DAYS, SLOTS, 2, 4, channels, WIDE), unit.dtype),
            pltpu.VMEM((64, 2 * F, WIDE), jnp.float32),
            pltpu.VMEM((64, WIDE, WIDE), jnp.float32),
            pltpu.VMEM((WIDE, 2 * F), jnp.float32),
            pltpu.VMEM((2 * WIDE, 2 * F), jnp.bfloat16),
            pltpu.VMEM((64, WIDE), jnp.float32),
            pltpu.SemaphoreType.DMA((count, 12)),
            pltpu.SemaphoreType.DMA((count, 15)),
            pltpu.SemaphoreType.DMA((count, 2)),
            pltpu.SemaphoreType.DMA,
        ],
        compiler_params=pltpu.CompilerParams(collective_id=0, has_side_effects=True, vmem_limit_bytes=44 << 20),
        name="correlate",
    )(unit, tables)


def per_device(spectra, validity):
    return correlate(own_unit(spectra, validity), jnp.asarray(lag_tables()))


def solution(mesh):
    placed = (P("day", None, ("col", "row"), None), P("day", ("col", "row")))
    return jax.shard_map(
        per_device, mesh=mesh, in_specs=placed, out_specs=P("row", "col", "day"), check_vma=False
    )
```

```python
import math

import jax
import jax.numpy as jnp
import numpy as np
from jax import lax
from jax.experimental import pallas as pl
from jax.experimental.pallas import tpu as pltpu
from jax.sharding import PartitionSpec as P

F = 256
LAGS = 512
ROWS, COLS, DAYS = 4, 8, 4
PACK = 4
GROUPS = F // PACK
SLOTS = GROUPS + 1
WIDE = 128
CHUNKS = "A5 B5 A6 B6 A6 B5 A5 B5 A5 B5 A5 B4 A3"
KINDS = [name[0] for name in CHUNKS.split()]
SIZES = [int(name[1:]) for name in CHUNKS.split()]
IDLE = (1, 1, 2, 1, 0, 1)
ORDER = (0, 2, 1, 3)
MESH = pl.DeviceIdType.MESH
NT = (((1,), (1,)), ((), ()))


def lag_tables():
    lag = np.arange(LAGS) - LAGS // 2
    freq = np.arange(F)
    phase = 2.0 * math.pi / (2 * F) * np.mod(lag[:, None] * freq[None, :], 2 * F)
    both = np.stack([np.cos(phase), -np.sin(phase)]) / math.sqrt(F)
    both = both.reshape(2, DAYS, LAGS // DAYS, PACK, GROUPS).transpose(1, 2, 4, 3, 0)
    return both.reshape(DAYS, LAGS // DAYS, 2 * F).astype(np.float32)


def own_unit(spectra, validity):
    windows, _, channels, _ = spectra.shape
    flags = validity.astype(jnp.bfloat16)
    cleaned = spectra * flags[:, None, :, None]
    split = cleaned.reshape(windows, 2, channels, PACK, GROUPS)
    packed = jnp.transpose(split, (4, 2, 3, 1, 0)).reshape(GROUPS, channels, WIDE)
    first = jnp.pad(flags.T, ((0, 0), (0, WIDE - windows)))
    return jnp.concatenate([first[None], packed])


def swap8(block):
    return jnp.swapaxes(block, 0, 1)


def correlate_kernel(unit, tables, out, near, full, stack, partial, exact, table, inverse, recv, sent, here, table_sem):
    row, col, day = lax.axis_index("row"), lax.axis_index("col"), lax.axis_index("day")
    core, x_hi, x_lo, y = row % 2, row // 2, col % 2, col // 2
    sibling = {"row": row + 1 - 2 * core}
    opposite = {"row": (row + 2) % ROWS}
    partner = {"col": col + 1 - 2 * x_lo}
    up_y, down_y = {"col": (col + 2) % COLS}, {"col": (col + COLS - 2) % COLS}
    days = [{"day": (day + step) % DAYS} for step in range(DAYS)]
    offset = (y + 4 - row) % 4
    home = offset == 0
    away = offset != 0
    beside = jnp.logical_or(offset == 1, offset == 3)
    far = offset == 2
    relay_up = jnp.logical_and(core == 1, offset == 1)
    relay_down = jnp.logical_and(core == 0, offset == 3)
    home_chip = x_hi == y // 2
    other_chip = x_hi != y // 2
    home_sibling = jnp.logical_and(home_chip, away)

    barrier = pltpu.get_barrier_semaphore()
    for peer in (sibling, opposite, partner, up_y, down_y, *days[1:]):
        pl.semaphore_signal(barrier, inc=1, device_id=peer, device_id_type=MESH)

    table_copy = pltpu.make_async_copy(tables.at[day], exact, table_sem)
    table_copy.start()

    count = len(SIZES)
    spans = [pl.ds(sum(SIZES[:k]), SIZES[k]) for k in range(count)]
    mine, theirs = pl.ds(2 * core, 2), pl.ds(2 - 2 * core, 2)
    all_units, both, later = pl.ds(0, 4), pl.ds(0, 2), pl.ds(1, DAYS - 1)
    pending = [[] for _ in range(count)]

    def act(when, body):
        if when is None:
            body()
        else:
            pl.when(when)(body)

    def send(k, src, dst, slot, peer, when=None, extra=0):
        def make():
            return pltpu.make_async_remote_copy(
                src_ref=src, dst_ref=dst, send_sem=sent.at[k, slot + extra], recv_sem=recv.at[k, slot],
                device_id=peer, device_id_type=MESH)

        act(when, lambda: make().start())
        pending[k].append((make, when))

    def arrive(k, dst, slot, when=None):
        act(when, lambda: pltpu.make_async_copy(dst, dst, recv.at[k, slot]).wait())

    def sent_all(k):
        for make, when in pending[k]:
            act(when, lambda make=make: make().wait_send())

    def n_at(k, d, part=all_units):
        return near.at[d, spans[k], part]

    def f_at(k, d, side, part=all_units):
        return full.at[d, spans[k], side, part]

    def day_sends(k, block, place, slot, when=None):
        for step in (1, 3, 2):
            send(k, block, place(DAYS - step), slot + step - 1, days[step], when)

    def day_arrivals(k, place, slot, when=None):
        for step in (1, 3, 2):
            arrive(k, place(DAYS - step), slot + step - 1, when)

    def start_units(k):
        place = near.at[0, spans[k], 2 * core + x_hi]
        send(k, unit.at[spans[k]], place, 0, opposite)
        copy = pltpu.make_async_copy(unit.at[spans[k]], place, here.at[k, 0])
        copy.start()
        return copy

    def spread_units(k):
        arrive(k, near.at[0, spans[k], 2 * core + 1 - x_hi], 0)
        copies[k].wait()
        block = n_at(k, 0, mine)
        send(k, block, block, 1, sibling)
        day_sends(k, block, lambda d: n_at(k, d, mine), 2, other_chip)

    def first_spread(k):
        arrive(k, n_at(k, 0, theirs), 1)
        block, place = n_at(k, 0), f_at(k, 0, x_lo)

        @pl.when(home)
        def _():
            copy = pltpu.make_async_copy(block, place, here.at[k, 1])
            copy.start()
            copy.wait()

        if KINDS[k] == "A":
            send(k, block, place, 6, up_y, home)
            send(k, block, place, 6, down_y, home, extra=6)
        else:
            send(k, block, place, 6, partner, home)

    def own_day(k):
        if KINDS[k] == "A":
            block = f_at(k, 0, x_lo)
            arrive(k, block, 6, away)
            send(k, block, block, 6, up_y, relay_up)
            send(k, block, block, 6, down_y, relay_down)
            day_sends(k, block, lambda d: f_at(k, d, x_lo), 7)
            send(k, block, block, 10, partner)
        else:
            arrive(k, f_at(k, 0, 1 - x_lo), 6, home)
            block = f_at(k, 0, both)
            day_sends(k, block, lambda d: f_at(k, d, both), 7, home)
            send(k, block, block, 10, up_y, home)
            send(k, block, block, 10, down_y, home, extra=3)

    def later_days(k):
        day_arrivals(k, lambda d: n_at(k, d, mine), 2, other_chip)
        block = n_at(k, later, mine)
        send(k, block, block, 5, sibling, other_chip)
        if KINDS[k] == "A":
            day_arrivals(k, lambda d: f_at(k, d, x_lo), 7)
            block = f_at(k, later, x_lo)
            send(k, block, block, 11, partner)
        else:
            day_arrivals(k, lambda d: f_at(k, d, both), 7, home)
            if KINDS[k] == "B":
                block = f_at(k, later, both)
                send(k, block, block, 11, up_y, home)
                send(k, block, block, 11, down_y, home, extra=3)
        block, place = f_at(k, later, x_lo), n_at(k, later)
        send(k, block, place, 5, sibling, home)
        act(home, lambda: pltpu.make_async_copy(block, place, here.at[k, 0]).start())

    def relay_own(k):
        if KINDS[k] != "A":
            relay(k, f_at(k, 0, both), 10)
        if KINDS[k] == "M":
            day_sends(k, f_at(k, 0, both), lambda d: f_at(k, d, both), 7, beside)

    def relay_later(k):
        if KINDS[k] == "B":
            relay(k, f_at(k, later, both), 11)
        if KINDS[k] == "M":
            arrive(k, f_at(k, 0, both), 10, far)
            day_sends(k, f_at(k, 0, both), lambda d: f_at(k, d, both), 7, far)

    def relay(k, block, slot):
        arrive(k, block, slot, beside)
        send(k, block, block, slot, up_y, relay_up)
        send(k, block, block, slot, down_y, relay_down)

    def finish(k):
        arrive(k, n_at(k, later, theirs), 5, other_chip)
        arrive(k, n_at(k, later), 5, home_sibling)
        act(home, lambda: pltpu.make_async_copy(f_at(k, later, x_lo), n_at(k, later), here.at[k, 0]).wait())
        if KINDS[k] == "A":
            arrive(k, f_at(k, 0, 1 - x_lo), 10)
            arrive(k, f_at(k, later, 1 - x_lo), 11)
        elif KINDS[k] == "B":
            arrive(k, f_at(k, 0, both), 10, far)
            arrive(k, f_at(k, later, both), 11, far)
        else:
            day_arrivals(k, lambda d: f_at(k, d, both), 7, away)

    lane = lax.broadcasted_iota(jnp.int32, (64, 2 * WIDE), 1)
    real = (lane // 16) % 2 == 0
    place = (lax.broadcasted_iota(jnp.int32, (1, 2 * WIDE), 1) // 32) % PACK
    masks = [jnp.where(place == at, 1.0, 0.0).astype(jnp.bfloat16) for at in range(PACK)]

    def columns(d, slot):
        return jnp.concatenate([near[d, slot, v] for v in ORDER], axis=0)

    def rows(d, slot):
        return jnp.concatenate([full[d, slot, side, v] for side in range(2) for v in ORDER], axis=0)

    def pair_counts():
        total = jnp.zeros((64, WIDE), jnp.float32)
        for d in range(DAYS):
            total += lax.dot_general(columns(d, 0), rows(d, 0), NT, preferred_element_type=jnp.float32)
        inverse[...] = 1.0 / jnp.maximum(total, 1.0)

    def stack_group(group):
        slot = group + 1
        total = None
        for pair in range(DAYS // 2):
            col = jnp.concatenate([columns(2 * pair, slot), columns(2 * pair + 1, slot)], axis=1)
            row = jnp.concatenate([rows(2 * pair, slot), rows(2 * pair + 1, slot)], axis=1)
            wide = col.astype(jnp.float32)
            swapped = jnp.where(real, -pltpu.roll(wide, 2 * WIDE - 16, 1), pltpu.roll(wide, 16, 1))
            swapped = swapped.astype(jnp.bfloat16)
            left = jnp.concatenate([side * mask for mask in masks for side in (col, swapped)], axis=0)
            term = lax.dot_general(left, row, NT, preferred_element_type=jnp.float32)
            total = term if total is None else total + term
        total = total.reshape(8, 64, WIDE)
        start = group * 8
        for at in range(0, 64, 8):
            stack[at : at + 8, pl.ds(start, 8), :] = swap8(total[:, at : at + 8, :])

    def split_table():
        table_copy.wait()
        high = exact[...].astype(jnp.bfloat16)
        table[:WIDE] = high
        table[WIDE:] = (exact[...] - high.astype(jnp.float32)).astype(jnp.bfloat16)

    def half_lags(j, half):
        span = pl.ds(half * F, F)
        values = stack[j, span, :]
        high = values.astype(jnp.bfloat16)
        low = (values - high.astype(jnp.float32)).astype(jnp.bfloat16)
        first = jnp.dot(table[:, span], high, preferred_element_type=jnp.float32)
        second = jnp.dot(table[:WIDE, span], low, preferred_element_type=jnp.float32)
        return first[:WIDE] + first[WIDE:] + second

    def first_half(group):
        for at in range(8):
            partial[group * 8 + at] = half_lags(group * 8 + at, 0)

    def second_half(group):
        done = []
        for at in range(8):
            j = group * 8 + at
            done.append(((partial[j] + half_lags(j, 1)) * inverse[pl.ds(j, 1), :]).T)
        start = pl.multiple_of(group * 8, 8)
        for at in range(0, WIDE, 8):
            out[at : at + 8, pl.ds(start, 8), :] = swap8(jnp.stack([d[at : at + 8] for d in done]))

    def repeat(body, first, times):
        def step(at, _):
            body(at)
            return 0

        lax.fori_loop(first, first + times, step, 0)

    work = []

    def ready(k):
        if k == 0:
            work.append(pair_counts)
        first, last = max(sum(SIZES[:k]) - 1, 0), sum(SIZES[: k + 1]) - 1
        work.append(lambda: [stack_group(at) for at in range(first, last)])
        if last == GROUPS // 2:
            work.append(split_table)
            for at in range(0, 8, 2):
                work.append(lambda first=at: repeat(first_half, first, 2))

    pl.semaphore_wait(barrier, 8)
    copies = [start_units(k) for k in range(count)]
    stages = [spread_units]
    for idle, stage in zip(IDLE, (first_spread, own_day, later_days, relay_own, relay_later, finish)):
        stages += [None] * idle + [stage]
    for step in range(count + len(stages) - 1):
        for at in reversed(range(len(stages))):
            if stages[at] and 0 <= step - at < count:
                stages[at](step - at)
                if work:
                    work.pop(0)()
        done = step + 1 - len(stages)
        if 0 <= done < count:
            ready(done)
        if 0 < done < count:
            sent_all(done - 1)
    for item in work:
        item()
    repeat(second_half, 0, 8)
    sent_all(count - 1)


def correlate(unit, tables):
    count = len(SIZES)
    channels = unit.shape[1]
    vmem = pl.BlockSpec(memory_space=pltpu.VMEM)
    return pl.pallas_call(
        correlate_kernel,
        out_shape=pltpu.VMEM((WIDE, 64, WIDE), jnp.float32),
        in_specs=[vmem, pl.BlockSpec(memory_space=pl.ANY)],
        out_specs=vmem,
        scratch_shapes=[
            pltpu.VMEM((DAYS, SLOTS, 4, channels, WIDE), unit.dtype),
            pltpu.VMEM((DAYS, SLOTS, 2, 4, channels, WIDE), unit.dtype),
            pltpu.VMEM((64, 2 * F, WIDE), jnp.float32),
            pltpu.VMEM((64, WIDE, WIDE), jnp.float32),
            pltpu.VMEM((WIDE, 2 * F), jnp.float32),
            pltpu.VMEM((2 * WIDE, 2 * F), jnp.bfloat16),
            pltpu.VMEM((64, WIDE), jnp.float32),
            pltpu.SemaphoreType.DMA((count, 12)),
            pltpu.SemaphoreType.DMA((count, 15)),
            pltpu.SemaphoreType.DMA((count, 2)),
            pltpu.SemaphoreType.DMA,
        ],
        compiler_params=pltpu.CompilerParams(collective_id=0, has_side_effects=True, vmem_limit_bytes=44 << 20),
        name="correlate",
    )(unit, tables)


def per_device(spectra, validity):
    return correlate(own_unit(spectra, validity), jnp.asarray(lag_tables()))


def solution(mesh):
    placed = (P("day", None, ("col", "row"), None), P("day", ("col", "row")))
    return jax.shard_map(
        per_device, mesh=mesh, in_specs=placed, out_specs=P("row", "col", "day"), check_vma=False
    )
```

```python
import math

import jax
import jax.numpy as jnp
import numpy as np
from jax import lax
from jax.experimental import pallas as pl
from jax.experimental.pallas import tpu as pltpu
from jax.sharding import PartitionSpec as P

F = 256
LAGS = 512
ROWS, COLS, DAYS = 4, 8, 4
PACK = 4
GROUPS = F // PACK
SLOTS = GROUPS + 1
WIDE = 128
CHUNKS = "B5 A5 M5 B5 A5 M4 B4 A5 M5 B5 A5 B5 A4 A3"
KINDS = [name[0] for name in CHUNKS.split()]
SIZES = [int(name[1:]) for name in CHUNKS.split()]
IDLE = (1, 1, 1, 1, 1, 0, 1, 1)
ORDER = (0, 2, 1, 3)
MESH = pl.DeviceIdType.MESH
NT = (((1,), (1,)), ((), ()))


def lag_tables():
    lag = np.arange(LAGS) - LAGS // 2
    freq = np.arange(F)
    phase = 2.0 * math.pi / (2 * F) * np.mod(lag[:, None] * freq[None, :], 2 * F)
    both = np.stack([np.cos(phase), -np.sin(phase)]) / math.sqrt(F)
    both = both.reshape(2, DAYS, LAGS // DAYS, PACK, GROUPS).transpose(1, 2, 4, 3, 0)
    return both.reshape(DAYS, LAGS // DAYS, 2 * F).astype(np.float32)


def pack_groups(spectra):
    windows, _, channels, _ = spectra.shape
    split = spectra.reshape(windows, 2, channels, PACK, GROUPS)
    return jnp.transpose(split, (4, 2, 3, 1, 0)).reshape(GROUPS, channels, WIDE)


def swap8(block):
    return jnp.swapaxes(block, 0, 1)


def correlate_kernel(groups, validity, tables, out, near, full, stack, partial, exact, table, inverse, recv, sent, here, table_sem):
    row, col, day = lax.axis_index("row"), lax.axis_index("col"), lax.axis_index("day")
    core, x_hi, x_lo, y = row % 2, row // 2, col % 2, col // 2
    sibling = {"row": row + 1 - 2 * core}
    opposite = {"row": (row + 2) % ROWS}
    partner = {"col": col + 1 - 2 * x_lo}
    up_y, down_y = {"col": (col + 2) % COLS}, {"col": (col + COLS - 2) % COLS}
    days = [{"day": (day + step) % DAYS} for step in range(DAYS)]
    offset = (y + 4 - row) % 4
    home = offset == 0
    away = offset != 0
    beside = jnp.logical_or(offset == 1, offset == 3)
    far = offset == 2
    relay_up = jnp.logical_and(core == 1, offset == 1)
    relay_down = jnp.logical_and(core == 0, offset == 3)
    home_chip = x_hi == y // 2
    other_chip = x_hi != y // 2
    home_sibling = jnp.logical_and(home_chip, away)

    barrier = pltpu.get_barrier_semaphore()
    for peer in (sibling, opposite, partner, up_y, down_y, *days[1:]):
        pl.semaphore_signal(barrier, inc=1, device_id=peer, device_id_type=MESH)

    table_copy = pltpu.make_async_copy(tables.at[day], exact, table_sem)
    table_copy.start()

    count = len(SIZES)
    spans = [pl.ds(sum(SIZES[:k]), SIZES[k]) for k in range(count)]
    mine, theirs = pl.ds(2 * core, 2), pl.ds(2 - 2 * core, 2)
    my_unit = 2 * core + x_hi
    all_units, both, later = pl.ds(0, 4), pl.ds(0, 2), pl.ds(1, DAYS - 1)
    pending = [[] for _ in range(count)]

    def act(when, body):
        if when is None:
            body()
        else:
            pl.when(when)(body)

    def send(k, src, dst, slot, peer, when=None, extra=0):
        def make():
            return pltpu.make_async_remote_copy(
                src_ref=src, dst_ref=dst, send_sem=sent.at[k, slot + extra], recv_sem=recv.at[k, slot],
                device_id=peer, device_id_type=MESH)

        act(when, lambda: make().start())
        pending[k].append((make, when))

    def arrive(k, dst, slot, when=None):
        act(when, lambda: pltpu.make_async_copy(dst, dst, recv.at[k, slot]).wait())

    def sent_all(k):
        for make, when in pending[k]:
            act(when, lambda make=make: make().wait_send())

    def n_at(k, d, part=all_units):
        return near.at[d, spans[k], part]

    def f_at(k, d, side, part=all_units):
        return full.at[d, spans[k], side, part]

    def day_sends(k, place, slot, when=None):
        send(k, place(0), place(DAYS - 1), slot, days[1], when)
        send(k, place(0), place(1), slot + 2, days[DAYS - 1], when)

    def day_forwards(k, place, half, slot, when=None):
        arrive(k, place(DAYS - 1), slot, when)
        send(k, half(DAYS - 1, 0), half(2, 0), slot + 1, days[1], when)
        arrive(k, place(1), slot + 2, when)
        send(k, half(1, 1), half(2, 1), 12 if slot == 2 else 13, days[DAYS - 1], when)

    def day_arrivals(k, half, slot, when=None):
        arrive(k, half(2, 0), slot + 1, when)
        arrive(k, half(2, 1), 12 if slot == 2 else 13, when)

    def near_blocks(k):
        return lambda d: n_at(k, d, mine), lambda d, part: n_at(k, d, pl.ds(2 * core + part, 1))

    def side_blocks(k):
        return lambda d: f_at(k, d, x_lo), lambda d, part: f_at(k, d, x_lo, pl.ds(2 * part, 2))

    def full_blocks(k):
        return lambda d: f_at(k, d, both), lambda d, part: f_at(k, d, part)

    def clean_unit():
        windows, channels = validity.shape
        lanes = lax.broadcasted_iota(jnp.int32, (windows, WIDE), 1) % windows
        spread = (lanes == lax.broadcasted_iota(jnp.int32, (windows, WIDE), 0)).astype(jnp.bfloat16)
        flags = validity[...].astype(jnp.float32).astype(jnp.bfloat16)
        flags = lax.dot_general(flags, spread, (((0,), (0,)), ((), ())), preferred_element_type=jnp.float32)
        first = lax.broadcasted_iota(jnp.int32, (channels, WIDE), 1) < windows
        near[0, 0, my_unit] = jnp.where(first, flags, 0.0).astype(jnp.bfloat16)
        flags = flags.astype(jnp.bfloat16)
        for at in range(GROUPS):
            near[0, at + 1, my_unit] = groups[at] * flags

    def start_units(k):
        place = near.at[0, spans[k], my_unit]
        send(k, place, place, 0, opposite)

    def spread_units(k):
        arrive(k, near.at[0, spans[k], 2 * core + 1 - x_hi], 0)
        block = n_at(k, 0, mine)
        send(k, block, block, 1, sibling)
        day_sends(k, near_blocks(k)[0], 2, other_chip)

    def first_spread(k):
        arrive(k, n_at(k, 0, theirs), 1)
        block, place = n_at(k, 0), f_at(k, 0, x_lo)

        @pl.when(home)
        def _():
            copy = pltpu.make_async_copy(block, place, here.at[k, 1])
            copy.start()
            copy.wait()

        if KINDS[k] == "A":
            send(k, block, place, 6, up_y, home)
            send(k, block, place, 6, down_y, home, extra=8)
        else:
            send(k, block, place, 6, partner, home)

    def own_day(k):
        if KINDS[k] == "A":
            block = f_at(k, 0, x_lo)
            arrive(k, block, 6, away)
            send(k, block, block, 6, up_y, relay_up)
            send(k, block, block, 6, down_y, relay_down)
            day_sends(k, side_blocks(k)[0], 7)
            send(k, block, block, 10, partner)
        else:
            arrive(k, f_at(k, 0, 1 - x_lo), 6, home)
            block = f_at(k, 0, both)
            day_sends(k, full_blocks(k)[0], 7, home)
            send(k, block, block, 10, up_y, home)
            send(k, block, block, 10, down_y, home, extra=5)

    def beside_days(k):
        day_forwards(k, *near_blocks(k), 2, other_chip)
        if KINDS[k] == "A":
            day_forwards(k, *side_blocks(k), 7)
        else:
            day_forwards(k, *full_blocks(k), 7, home)

    def later_days(k):
        day_arrivals(k, near_blocks(k)[1], 2, other_chip)
        block = n_at(k, later, mine)
        send(k, block, block, 5, sibling, other_chip)
        if KINDS[k] == "A":
            day_arrivals(k, side_blocks(k)[1], 7)
            block = f_at(k, later, x_lo)
            send(k, block, block, 11, partner)
        else:
            day_arrivals(k, full_blocks(k)[1], 7, home)
            if KINDS[k] == "B":
                block = f_at(k, later, both)
                send(k, block, block, 11, up_y, home)
                send(k, block, block, 11, down_y, home, extra=5)
        block, place = f_at(k, later, x_lo), n_at(k, later)
        send(k, block, place, 5, sibling, home)
        act(home, lambda: pltpu.make_async_copy(block, place, here.at[k, 0]).start())

    def relay_own(k):
        if KINDS[k] != "A":
            relay(k, f_at(k, 0, both), 10)
        if KINDS[k] == "M":
            day_sends(k, full_blocks(k)[0], 7, beside)

    def relay_later(k):
        if KINDS[k] == "B":
            relay(k, f_at(k, later, both), 11)
        if KINDS[k] == "M":
            arrive(k, f_at(k, 0, both), 10, far)
            day_sends(k, full_blocks(k)[0], 7, far)

    def last_days(k):
        if KINDS[k] == "M":
            day_forwards(k, *full_blocks(k), 7, away)

    def relay(k, block, slot):
        arrive(k, block, slot, beside)
        send(k, block, block, slot, up_y, relay_up)
        send(k, block, block, slot, down_y, relay_down)

    def finish(k):
        arrive(k, n_at(k, later, theirs), 5, other_chip)
        arrive(k, n_at(k, later), 5, home_sibling)
        act(home, lambda: pltpu.make_async_copy(f_at(k, later, x_lo), n_at(k, later), here.at[k, 0]).wait())
        if KINDS[k] == "A":
            arrive(k, f_at(k, 0, 1 - x_lo), 10)
            arrive(k, f_at(k, later, 1 - x_lo), 11)
        elif KINDS[k] == "B":
            arrive(k, f_at(k, 0, both), 10, far)
            arrive(k, f_at(k, later, both), 11, far)
        else:
            day_arrivals(k, full_blocks(k)[1], 7, away)

    lane = lax.broadcasted_iota(jnp.int32, (64, 2 * WIDE), 1)
    real = (lane // 16) % 2 == 0
    place = (lax.broadcasted_iota(jnp.int32, (1, 2 * WIDE), 1) // 32) % PACK
    masks = [jnp.where(place == at, 1.0, 0.0).astype(jnp.bfloat16) for at in range(PACK)]

    def columns(d, slot):
        return jnp.concatenate([near[d, slot, v] for v in ORDER], axis=0)

    def rows(d, slot):
        return jnp.concatenate([full[d, slot, side, v] for side in range(2) for v in ORDER], axis=0)

    def pair_counts():
        total = jnp.zeros((64, WIDE), jnp.float32)
        for d in range(DAYS):
            total += lax.dot_general(columns(d, 0), rows(d, 0), NT, preferred_element_type=jnp.float32)
        inverse[...] = 1.0 / jnp.maximum(total, 1.0)

    def stack_group(group):
        slot = group + 1
        total = None
        for pair in range(DAYS // 2):
            col = jnp.concatenate([columns(2 * pair, slot), columns(2 * pair + 1, slot)], axis=1)
            row = jnp.concatenate([rows(2 * pair, slot), rows(2 * pair + 1, slot)], axis=1)
            wide = col.astype(jnp.float32)
            swapped = jnp.where(real, -pltpu.roll(wide, 2 * WIDE - 16, 1), pltpu.roll(wide, 16, 1))
            swapped = swapped.astype(jnp.bfloat16)
            left = jnp.concatenate([side * mask for mask in masks for side in (col, swapped)], axis=0)
            term = lax.dot_general(left, row, NT, preferred_element_type=jnp.float32)
            total = term if total is None else total + term
        total = total.reshape(8, 64, WIDE)
        start = group * 8
        for at in range(0, 64, 8):
            stack[at : at + 8, pl.ds(start, 8), :] = swap8(total[:, at : at + 8, :])

    def split_table():
        table_copy.wait()
        high = exact[...].astype(jnp.bfloat16)
        table[:WIDE] = high
        table[WIDE:] = (exact[...] - high.astype(jnp.float32)).astype(jnp.bfloat16)

    def half_lags(j, half):
        span = pl.ds(half * F, F)
        values = jnp.concatenate([stack[j, span, :], stack[j + 1, span, :]], axis=1)
        high = values.astype(jnp.bfloat16)
        low = (values - high.astype(jnp.float32)).astype(jnp.bfloat16)
        first = jnp.dot(table[:, span], high, preferred_element_type=jnp.float32)
        second = jnp.dot(table[:WIDE, span], low, preferred_element_type=jnp.float32)
        lags = first[:WIDE] + first[WIDE:] + second
        return lags[:, :WIDE], lags[:, WIDE:]

    def first_half(group):
        for at in range(0, 8, 2):
            j = group * 8 + at
            partial[j], partial[j + 1] = half_lags(j, 0)

    def second_half(group):
        done = []
        for at in range(0, 8, 2):
            j = group * 8 + at
            for k, lags in enumerate(half_lags(j, 1)):
                done.append(((partial[j + k] + lags) * inverse[pl.ds(j + k, 1), :]).T)
        start = pl.multiple_of(group * 8, 8)
        for at in range(0, WIDE, 8):
            out[at : at + 8, pl.ds(start, 8), :] = swap8(jnp.stack([d[at : at + 8] for d in done]))

    def repeat(body, first, times):
        def step(at, _):
            body(at)
            return 0

        lax.fori_loop(first, first + times, step, 0)

    work = []

    def ready(k):
        if k == 0:
            work.append(pair_counts)
        first, last = max(sum(SIZES[:k]) - 1, 0), sum(SIZES[: k + 1]) - 1
        work.append(lambda: [stack_group(at) for at in range(first, last)])
        if last == GROUPS // 2:
            work.append(split_table)
            for at in range(0, 8, 2):
                work.append(lambda first=at: repeat(first_half, first, 2))

    clean_unit()
    pl.semaphore_wait(barrier, 8)
    for k in range(count):
        start_units(k)
    stages = [spread_units]
    order = (first_spread, own_day, beside_days, later_days, relay_own, relay_later, last_days, finish)
    for idle, stage in zip(IDLE, order):
        stages += [None] * idle + [stage]
    for step in range(count + len(stages) - 1):
        for at in range(len(stages)):
            if stages[at] and 0 <= step - at < count:
                stages[at](step - at)
                if work:
                    work.pop(0)()
        done = step + 1 - len(stages)
        if 0 <= done < count:
            ready(done)
        if 0 < done < count:
            sent_all(done - 1)
    for item in work:
        item()
    repeat(second_half, 0, 8)
    sent_all(count - 1)


def correlate(groups, validity, tables):
    count = len(SIZES)
    channels = groups.shape[1]
    vmem = pl.BlockSpec(memory_space=pltpu.VMEM)
    return pl.pallas_call(
        correlate_kernel,
        out_shape=pltpu.VMEM((WIDE, 64, WIDE), jnp.float32),
        in_specs=[vmem, vmem, pl.BlockSpec(memory_space=pltpu.HBM)],
        out_specs=vmem,
        scratch_shapes=[
            pltpu.VMEM((DAYS, SLOTS, 4, channels, WIDE), groups.dtype),
            pltpu.VMEM((DAYS, SLOTS, 2, 4, channels, WIDE), groups.dtype),
            pltpu.VMEM((64, 2 * F, WIDE), jnp.float32),
            pltpu.VMEM((64, WIDE, WIDE), jnp.float32),
            pltpu.VMEM((WIDE, 2 * F), jnp.float32),
            pltpu.VMEM((2 * WIDE, 2 * F), jnp.bfloat16),
            pltpu.VMEM((64, WIDE), jnp.float32),
            pltpu.SemaphoreType.DMA((count, 14)),
            pltpu.SemaphoreType.DMA((count, 17)),
            pltpu.SemaphoreType.DMA((count, 2)),
            pltpu.SemaphoreType.DMA,
        ],
        compiler_params=pltpu.CompilerParams(collective_id=0, has_side_effects=True, vmem_limit_bytes=44 << 20),
        name="correlate",
    )(groups, validity, tables)


def per_device(spectra, validity):
    return correlate(pack_groups(spectra), validity, jnp.asarray(lag_tables()))


def solution(mesh):
    placed = (P("day", None, ("col", "row"), None), P("day", ("col", "row")))
    return jax.shard_map(
        per_device, mesh=mesh, in_specs=placed, out_specs=P("row", "col", "day"), check_vma=False
    )
```

```python
import math

import jax
import jax.numpy as jnp
import numpy as np
from jax import lax
from jax.experimental import pallas as pl
from jax.experimental.pallas import tpu as pltpu
from jax.sharding import PartitionSpec as P

F = 256
LAGS = 512
ROWS, COLS, DAYS = 4, 8, 4
PACK = 4
GROUPS = F // PACK
SLOTS = GROUPS + 1
WIDE = 128
CHUNKS = "B5 A5 M5 B5 A5 M4 B4 A5 M5 B5 A5 B5 A4 A3"
KINDS = [name[0] for name in CHUNKS.split()]
SIZES = [int(name[1:]) for name in CHUNKS.split()]
IDLE = (1, 1, 1, 1, 1, 0, 1, 1)
ORDER = (0, 2, 1, 3)
MESH = pl.DeviceIdType.MESH
NT = (((1,), (1,)), ((), ()))


def lag_tables():
    lag = np.arange(LAGS) - LAGS // 2
    freq = np.arange(F)
    phase = 2.0 * math.pi / (2 * F) * np.mod(lag[:, None] * freq[None, :], 2 * F)
    both = np.stack([np.cos(phase), -np.sin(phase)]) / math.sqrt(F)
    both = both.reshape(2, DAYS, LAGS // DAYS, PACK, GROUPS).transpose(1, 2, 4, 3, 0)
    return both.reshape(DAYS, LAGS // DAYS, 2 * F).astype(np.float32)


def pack_groups(spectra):
    windows, _, channels, _ = spectra.shape
    split = spectra.reshape(windows, 2, channels, PACK, GROUPS)
    return jnp.transpose(split, (4, 2, 3, 1, 0)).reshape(GROUPS, channels, WIDE)


def swap8(block):
    return jnp.swapaxes(block, 0, 1)


def correlate_kernel(
    groups, validity, tables, out, near, full, stack, partial, exact, table, inverse, usable, recv, sent, here, fetch
):
    row, col, day = lax.axis_index("row"), lax.axis_index("col"), lax.axis_index("day")
    core, x_hi, x_lo, y = row % 2, row // 2, col % 2, col // 2
    sibling = {"row": row + 1 - 2 * core}
    opposite = {"row": (row + 2) % ROWS}
    partner = {"col": col + 1 - 2 * x_lo}
    up_y, down_y = {"col": (col + 2) % COLS}, {"col": (col + COLS - 2) % COLS}
    days = [{"day": (day + step) % DAYS} for step in range(DAYS)]
    offset = (y + 4 - row) % 4
    home = offset == 0
    away = offset != 0
    beside = jnp.logical_or(offset == 1, offset == 3)
    far = offset == 2
    relay_up = jnp.logical_and(core == 1, offset == 1)
    relay_down = jnp.logical_and(core == 0, offset == 3)
    home_chip = x_hi == y // 2
    other_chip = x_hi != y // 2
    home_sibling = jnp.logical_and(home_chip, away)

    barrier = pltpu.get_barrier_semaphore()
    for peer in (sibling, opposite, partner, up_y, down_y, *days[1:]):
        pl.semaphore_signal(barrier, inc=1, device_id=peer, device_id_type=MESH)

    flag_copy = pltpu.make_async_copy(validity, usable, fetch.at[0])
    flag_copy.start()
    table_copy = pltpu.make_async_copy(tables.at[day], exact, fetch.at[1])
    table_copy.start()

    count = len(SIZES)
    spans = [pl.ds(sum(SIZES[:k]), SIZES[k]) for k in range(count)]
    mine, theirs = pl.ds(2 * core, 2), pl.ds(2 - 2 * core, 2)
    my_unit = 2 * core + x_hi
    all_units, both, later = pl.ds(0, 4), pl.ds(0, 2), pl.ds(1, DAYS - 1)
    pending = [[] for _ in range(count)]

    def act(when, body):
        if when is None:
            body()
        else:
            pl.when(when)(body)

    def send(k, src, dst, slot, peer, when=None, extra=0):
        def make():
            return pltpu.make_async_remote_copy(
                src_ref=src, dst_ref=dst, send_sem=sent.at[k, slot + extra], recv_sem=recv.at[k, slot],
                device_id=peer, device_id_type=MESH)

        act(when, lambda: make().start())
        pending[k].append((make, when))

    def arrive(k, dst, slot, when=None):
        act(when, lambda: pltpu.make_async_copy(dst, dst, recv.at[k, slot]).wait())

    def sent_all(k):
        for make, when in pending[k]:
            act(when, lambda make=make: make().wait_send())

    def n_at(k, d, part=all_units):
        return near.at[d, spans[k], part]

    def f_at(k, d, side, part=all_units):
        return full.at[d, spans[k], side, part]

    def day_sends(k, place, slot, when=None):
        send(k, place(0), place(DAYS - 1), slot, days[1], when)
        send(k, place(0), place(1), slot + 2, days[DAYS - 1], when)

    def day_forwards(k, place, half, slot, when=None):
        arrive(k, place(DAYS - 1), slot, when)
        send(k, half(DAYS - 1, 0), half(2, 0), slot + 1, days[1], when)
        arrive(k, place(1), slot + 2, when)
        send(k, half(1, 1), half(2, 1), 12 if slot == 2 else 13, days[DAYS - 1], when)

    def day_arrivals(k, half, slot, when=None):
        arrive(k, half(2, 0), slot + 1, when)
        arrive(k, half(2, 1), 12 if slot == 2 else 13, when)

    def near_blocks(k):
        return lambda d: n_at(k, d, mine), lambda d, part: n_at(k, d, pl.ds(2 * core + part, 1))

    def side_blocks(k):
        return lambda d: f_at(k, d, x_lo), lambda d, part: f_at(k, d, x_lo, pl.ds(2 * part, 2))

    def full_blocks(k):
        return lambda d: f_at(k, d, both), lambda d, part: f_at(k, d, part)

    def clean_unit():
        windows, channels = usable.shape
        flag_copy.wait()
        lanes = lax.broadcasted_iota(jnp.int32, (windows, WIDE), 1) % windows
        spread = (lanes == lax.broadcasted_iota(jnp.int32, (windows, WIDE), 0)).astype(jnp.bfloat16)
        flags = usable[...].astype(jnp.float32).astype(jnp.bfloat16)
        flags = lax.dot_general(flags, spread, (((0,), (0,)), ((), ())), preferred_element_type=jnp.float32)
        first = lax.broadcasted_iota(jnp.int32, (channels, WIDE), 1) < windows
        near[0, 0, my_unit] = jnp.where(first, flags, 0.0).astype(jnp.bfloat16)
        flags = flags.astype(jnp.bfloat16)
        for at in range(GROUPS):
            near[0, at + 1, my_unit] = groups[at] * flags

    def start_units(k):
        place = near.at[0, spans[k], my_unit]
        send(k, place, place, 0, opposite)

    def spread_units(k):
        arrive(k, near.at[0, spans[k], 2 * core + 1 - x_hi], 0)
        block = n_at(k, 0, mine)
        send(k, block, block, 1, sibling)
        day_sends(k, near_blocks(k)[0], 2, other_chip)

    def first_spread(k):
        arrive(k, n_at(k, 0, theirs), 1)
        block, place = n_at(k, 0), f_at(k, 0, x_lo)

        @pl.when(home)
        def _():
            copy = pltpu.make_async_copy(block, place, here.at[k, 1])
            copy.start()
            copy.wait()

        if KINDS[k] == "A":
            send(k, block, place, 6, up_y, home)
            send(k, block, place, 6, down_y, home, extra=8)
        else:
            send(k, block, place, 6, partner, home)

    def own_day(k):
        if KINDS[k] == "A":
            block = f_at(k, 0, x_lo)
            arrive(k, block, 6, away)
            send(k, block, block, 6, up_y, relay_up)
            send(k, block, block, 6, down_y, relay_down)
            day_sends(k, side_blocks(k)[0], 7)
            send(k, block, block, 10, partner)
        else:
            arrive(k, f_at(k, 0, 1 - x_lo), 6, home)
            block = f_at(k, 0, both)
            day_sends(k, full_blocks(k)[0], 7, home)
            send(k, block, block, 10, up_y, home)
            send(k, block, block, 10, down_y, home, extra=5)

    def beside_days(k):
        day_forwards(k, *near_blocks(k), 2, other_chip)
        if KINDS[k] == "A":
            day_forwards(k, *side_blocks(k), 7)
        else:
            day_forwards(k, *full_blocks(k), 7, home)

    def later_days(k):
        day_arrivals(k, near_blocks(k)[1], 2, other_chip)
        block = n_at(k, later, mine)
        send(k, block, block, 5, sibling, other_chip)
        if KINDS[k] == "A":
            day_arrivals(k, side_blocks(k)[1], 7)
            block = f_at(k, later, x_lo)
            send(k, block, block, 11, partner)
        else:
            day_arrivals(k, full_blocks(k)[1], 7, home)
            if KINDS[k] == "B":
                block = f_at(k, later, both)
                send(k, block, block, 11, up_y, home)
                send(k, block, block, 11, down_y, home, extra=5)
        block, place = f_at(k, later, x_lo), n_at(k, later)
        send(k, block, place, 5, sibling, home)
        act(home, lambda: pltpu.make_async_copy(block, place, here.at[k, 0]).start())

    def relay_own(k):
        if KINDS[k] != "A":
            relay(k, f_at(k, 0, both), 10)
        if KINDS[k] == "M":
            day_sends(k, full_blocks(k)[0], 7, beside)

    def relay_later(k):
        if KINDS[k] == "B":
            relay(k, f_at(k, later, both), 11)
        if KINDS[k] == "M":
            arrive(k, f_at(k, 0, both), 10, far)
            day_sends(k, full_blocks(k)[0], 7, far)

    def last_days(k):
        if KINDS[k] == "M":
            day_forwards(k, *full_blocks(k), 7, away)

    def relay(k, block, slot):
        arrive(k, block, slot, beside)
        send(k, block, block, slot, up_y, relay_up)
        send(k, block, block, slot, down_y, relay_down)

    def finish(k):
        arrive(k, n_at(k, later, theirs), 5, other_chip)
        arrive(k, n_at(k, later), 5, home_sibling)
        act(home, lambda: pltpu.make_async_copy(f_at(k, later, x_lo), n_at(k, later), here.at[k, 0]).wait())
        if KINDS[k] == "A":
            arrive(k, f_at(k, 0, 1 - x_lo), 10)
            arrive(k, f_at(k, later, 1 - x_lo), 11)
        elif KINDS[k] == "B":
            arrive(k, f_at(k, 0, both), 10, far)
            arrive(k, f_at(k, later, both), 11, far)
        else:
            day_arrivals(k, full_blocks(k)[1], 7, away)

    lane = lax.broadcasted_iota(jnp.int32, (64, 2 * WIDE), 1)
    real = (lane // 16) % 2 == 0
    place = (lax.broadcasted_iota(jnp.int32, (1, 2 * WIDE), 1) // 32) % PACK
    masks = [jnp.where(place == at, 1.0, 0.0).astype(jnp.bfloat16) for at in range(PACK)]

    def columns(d, slot):
        return jnp.concatenate([near[d, slot, v] for v in ORDER], axis=0)

    def rows(d, slot):
        return jnp.concatenate([full[d, slot, side, v] for side in range(2) for v in ORDER], axis=0)

    def pair_counts():
        total = jnp.zeros((64, WIDE), jnp.float32)
        for d in range(DAYS):
            total += lax.dot_general(columns(d, 0), rows(d, 0), NT, preferred_element_type=jnp.float32)
        inverse[...] = 1.0 / jnp.maximum(total, 1.0)

    def stack_group(group):
        slot = group + 1
        total = None
        for pair in range(DAYS // 2):
            col = jnp.concatenate([columns(2 * pair, slot), columns(2 * pair + 1, slot)], axis=1)
            row = jnp.concatenate([rows(2 * pair, slot), rows(2 * pair + 1, slot)], axis=1)
            wide = col.astype(jnp.float32)
            swapped = jnp.where(real, -pltpu.roll(wide, 2 * WIDE - 16, 1), pltpu.roll(wide, 16, 1))
            swapped = swapped.astype(jnp.bfloat16)
            left = jnp.concatenate([side * mask for mask in masks for side in (col, swapped)], axis=0)
            term = lax.dot_general(left, row, NT, preferred_element_type=jnp.float32)
            total = term if total is None else total + term
        total = total.reshape(8, 64, WIDE)
        start = group * 8
        for at in range(0, 64, 8):
            stack[at : at + 8, pl.ds(start, 8), :] = swap8(total[:, at : at + 8, :])

    def split_table():
        table_copy.wait()
        high = exact[...].astype(jnp.bfloat16)
        table[:WIDE] = high
        table[WIDE:] = (exact[...] - high.astype(jnp.float32)).astype(jnp.bfloat16)

    def half_lags(j, half):
        span = pl.ds(half * F, F)
        values = jnp.concatenate([stack[j, span, :], stack[j + 1, span, :]], axis=1)
        high = values.astype(jnp.bfloat16)
        low = (values - high.astype(jnp.float32)).astype(jnp.bfloat16)
        first = jnp.dot(table[:, span], high, preferred_element_type=jnp.float32)
        second = jnp.dot(table[:WIDE, span], low, preferred_element_type=jnp.float32)
        lags = first[:WIDE] + first[WIDE:] + second
        return lags[:, :WIDE], lags[:, WIDE:]

    def first_half(group):
        for at in range(0, 8, 2):
            j = group * 8 + at
            partial[j], partial[j + 1] = half_lags(j, 0)

    def second_half(group):
        done = []
        for at in range(0, 8, 2):
            j = group * 8 + at
            for k, lags in enumerate(half_lags(j, 1)):
                done.append(((partial[j + k] + lags) * inverse[pl.ds(j + k, 1), :]).T)
        start = pl.multiple_of(group * 8, 8)
        for at in range(0, WIDE, 8):
            out[at : at + 8, pl.ds(start, 8), :] = swap8(jnp.stack([d[at : at + 8] for d in done]))

    def repeat(body, first, times):
        def step(at, _):
            body(at)
            return 0

        lax.fori_loop(first, first + times, step, 0)

    work = []

    def ready(k):
        if k == 0:
            work.append(pair_counts)
        first, last = max(sum(SIZES[:k]) - 1, 0), sum(SIZES[: k + 1]) - 1
        work.append(lambda: [stack_group(at) for at in range(first, last)])
        if last == GROUPS // 2:
            work.append(split_table)
            for at in range(0, 8, 2):
                work.append(lambda first=at: repeat(first_half, first, 2))

    clean_unit()
    pl.semaphore_wait(barrier, 8)
    for k in range(count):
        start_units(k)
    stages = [spread_units]
    order = (first_spread, own_day, beside_days, later_days, relay_own, relay_later, last_days, finish)
    for idle, stage in zip(IDLE, order):
        stages += [None] * idle + [stage]
    for step in range(count + len(stages) - 1):
        for at in range(len(stages)):
            if stages[at] and 0 <= step - at < count:
                stages[at](step - at)
                if work:
                    work.pop(0)()
        done = step + 1 - len(stages)
        if 0 <= done < count:
            ready(done)
        if 0 < done < count:
            sent_all(done - 1)
    for item in work:
        item()
    repeat(second_half, 0, 8)
    sent_all(count - 1)


def correlate(groups, validity, tables):
    count = len(SIZES)
    channels = groups.shape[1]
    vmem, anywhere = pl.BlockSpec(memory_space=pltpu.VMEM), pl.BlockSpec(memory_space=pl.ANY)
    return pl.pallas_call(
        correlate_kernel,
        out_shape=pltpu.VMEM((WIDE, 64, WIDE), jnp.float32),
        in_specs=[vmem, anywhere, anywhere],
        out_specs=vmem,
        scratch_shapes=[
            pltpu.VMEM((DAYS, SLOTS, 4, channels, WIDE), groups.dtype),
            pltpu.VMEM((DAYS, SLOTS, 2, 4, channels, WIDE), groups.dtype),
            pltpu.VMEM((64, 2 * F, WIDE), jnp.float32),
            pltpu.VMEM((64, WIDE, WIDE), jnp.float32),
            pltpu.VMEM((WIDE, 2 * F), jnp.float32),
            pltpu.VMEM((2 * WIDE, 2 * F), jnp.bfloat16),
            pltpu.VMEM((64, WIDE), jnp.float32),
            pltpu.VMEM(validity.shape, validity.dtype),
            pltpu.SemaphoreType.DMA((count, 14)),
            pltpu.SemaphoreType.DMA((count, 17)),
            pltpu.SemaphoreType.DMA((count, 2)),
            pltpu.SemaphoreType.DMA((2,)),
        ],
        compiler_params=pltpu.CompilerParams(collective_id=0, has_side_effects=True, vmem_limit_bytes=58 << 20),
        name="correlate",
    )(groups, validity, tables)


def per_device(spectra, validity):
    return correlate(pltpu.with_memory_space_constraint(pack_groups(spectra), pltpu.VMEM), validity, jnp.asarray(lag_tables()))


def solution(mesh):
    placed = (P("day", None, ("col", "row"), None), P("day", ("col", "row")))
    return jax.shard_map(
        per_device, mesh=mesh, in_specs=placed, out_specs=P("row", "col", "day"), check_vma=False
    )
```

```python
import math

import jax
import jax.numpy as jnp
import numpy as np
from jax import lax
from jax.experimental import pallas as pl
from jax.experimental.pallas import tpu as pltpu
from jax.sharding import PartitionSpec as P

F = 256
LAGS = 512
ROWS, COLS, DAYS = 4, 8, 4
PACK = 4
GROUPS = F // PACK
SLOTS = GROUPS + 1
WIDE = 128
CHUNKS = "B4 A4 M4 B4 A4 M4 B4 A5 B4 A4 M4 B4 A4 B4 A4 A4"
KINDS = [name[0] for name in CHUNKS.split()]
SIZES = [int(name[1:]) for name in CHUNKS.split()]
IDLE = (1, 1, 1, 1, 1, 0, 1, 1)
ORDER = (0, 2, 1, 3)
MESH = pl.DeviceIdType.MESH
NT = (((1,), (1,)), ((), ()))


def lag_tables():
    lag = np.arange(LAGS) - LAGS // 2
    freq = np.arange(F)
    phase = 2.0 * math.pi / (2 * F) * np.mod(lag[:, None] * freq[None, :], 2 * F)
    both = np.stack([np.cos(phase), -np.sin(phase)]) / math.sqrt(F)
    both = both.reshape(2, DAYS, LAGS // DAYS, PACK, GROUPS).transpose(1, 2, 4, 3, 0)
    return both.reshape(DAYS, LAGS // DAYS, 2 * F).astype(np.float32)


def pack_groups(spectra):
    windows, _, channels, _ = spectra.shape
    split = jnp.transpose(spectra, (3, 2, 1, 0)).reshape(PACK, GROUPS, channels, 2 * windows)
    return jnp.transpose(split, (1, 2, 0, 3)).reshape(GROUPS, channels, WIDE)


def swap8(block):
    return jnp.swapaxes(block, 0, 1)


def correlate_kernel(
    groups, validity, tables, lags, near, full, stack, exact, table, inverse, usable, recv, sent, here, fetch
):
    row, col, day = lax.axis_index("row"), lax.axis_index("col"), lax.axis_index("day")
    core, x_hi, x_lo, y = row % 2, row // 2, col % 2, col // 2
    sibling = {"row": row + 1 - 2 * core}
    opposite = {"row": (row + 2) % ROWS}
    partner = {"col": col + 1 - 2 * x_lo}
    up_y, down_y = {"col": (col + 2) % COLS}, {"col": (col + COLS - 2) % COLS}
    days = [{"day": (day + step) % DAYS} for step in range(DAYS)]
    offset = (y + 4 - row) % 4
    home = offset == 0
    away = offset != 0
    beside = jnp.logical_or(offset == 1, offset == 3)
    far = offset == 2
    relay_up = jnp.logical_and(core == 1, offset == 1)
    relay_down = jnp.logical_and(core == 0, offset == 3)
    home_chip = x_hi == y // 2
    other_chip = x_hi != y // 2
    home_sibling = jnp.logical_and(home_chip, away)

    barrier = pltpu.get_barrier_semaphore()
    for peer in (sibling, opposite, partner, up_y, down_y, *days[1:]):
        pl.semaphore_signal(barrier, inc=1, device_id=peer, device_id_type=MESH)

    flag_copy = pltpu.make_async_copy(validity, usable, fetch.at[0])
    flag_copy.start()
    table_copy = pltpu.make_async_copy(tables.at[day], exact, fetch.at[1])
    table_copy.start()

    count = len(SIZES)
    spans = [pl.ds(sum(SIZES[:k]), SIZES[k]) for k in range(count)]
    mine, theirs = pl.ds(2 * core, 2), pl.ds(2 - 2 * core, 2)
    my_unit = 2 * core + x_hi
    all_units, both, later = pl.ds(0, 4), pl.ds(0, 2), pl.ds(1, DAYS - 1)
    pending = [[] for _ in range(count)]

    def act(when, body):
        if when is None:
            body()
        else:
            pl.when(when)(body)

    def send(k, src, dst, slot, peer, when=None, extra=0):
        def make():
            return pltpu.make_async_remote_copy(
                src_ref=src, dst_ref=dst, send_sem=sent.at[k, slot + extra], recv_sem=recv.at[k, slot],
                device_id=peer, device_id_type=MESH)

        act(when, lambda: make().start())
        pending[k].append((make, when))

    def arrive(k, dst, slot, when=None):
        act(when, lambda: pltpu.make_async_copy(dst, dst, recv.at[k, slot]).wait())

    def sent_all(k):
        for make, when in pending[k]:
            act(when, lambda make=make: make().wait_send())

    def n_at(k, d, part=all_units):
        return near.at[d, spans[k], part]

    def f_at(k, d, side, part=all_units):
        return full.at[d, spans[k], side, part]

    def day_sends(k, place, slot, when=None):
        send(k, place(0), place(DAYS - 1), slot, days[1], when)
        send(k, place(0), place(1), slot + 2, days[DAYS - 1], when)

    def day_forwards(k, place, half, slot, when=None):
        arrive(k, place(DAYS - 1), slot, when)
        send(k, half(DAYS - 1, 0), half(2, 0), slot + 1, days[1], when)
        arrive(k, place(1), slot + 2, when)
        send(k, half(1, 1), half(2, 1), 12 if slot == 2 else 13, days[DAYS - 1], when)

    def day_arrivals(k, half, slot, when=None):
        arrive(k, half(2, 0), slot + 1, when)
        arrive(k, half(2, 1), 12 if slot == 2 else 13, when)

    def near_blocks(k):
        return lambda d: n_at(k, d, mine), lambda d, part: n_at(k, d, pl.ds(2 * core + part, 1))

    def side_blocks(k):
        return lambda d: f_at(k, d, x_lo), lambda d, part: f_at(k, d, x_lo, pl.ds(2 * part, 2))

    def full_blocks(k):
        return lambda d: f_at(k, d, both), lambda d, part: f_at(k, d, part)

    def clean_unit():
        windows, channels = usable.shape
        flag_copy.wait()
        lanes = lax.broadcasted_iota(jnp.int32, (windows, WIDE), 1) % windows
        spread = (lanes == lax.broadcasted_iota(jnp.int32, (windows, WIDE), 0)).astype(jnp.bfloat16)
        flags = usable[...].astype(jnp.float32).astype(jnp.bfloat16)
        flags = lax.dot_general(flags, spread, (((0,), (0,)), ((), ())), preferred_element_type=jnp.float32)
        first = lax.broadcasted_iota(jnp.int32, (channels, WIDE), 1) < windows
        near[0, 0, my_unit] = jnp.where(first, flags, 0.0).astype(jnp.bfloat16)
        flags = flags.astype(jnp.bfloat16)
        for at in range(GROUPS):
            near[0, at + 1, my_unit] = groups[at] * flags

    def start_units(k):
        place = near.at[0, spans[k], my_unit]
        send(k, place, place, 0, opposite)

    def spread_units(k):
        arrive(k, near.at[0, spans[k], 2 * core + 1 - x_hi], 0)
        block = n_at(k, 0, mine)
        send(k, block, block, 1, sibling)
        day_sends(k, near_blocks(k)[0], 2, other_chip)

    def first_spread(k):
        arrive(k, n_at(k, 0, theirs), 1)
        block, place = n_at(k, 0), f_at(k, 0, x_lo)

        @pl.when(home)
        def _():
            copy = pltpu.make_async_copy(block, place, here.at[k, 1])
            copy.start()
            copy.wait()

        if KINDS[k] == "A":
            send(k, block, place, 6, up_y, home)
            send(k, block, place, 6, down_y, home, extra=8)
        else:
            send(k, block, place, 6, partner, home)

    def own_day(k):
        if KINDS[k] == "A":
            block = f_at(k, 0, x_lo)
            arrive(k, block, 6, away)
            send(k, block, block, 6, up_y, relay_up)
            send(k, block, block, 6, down_y, relay_down)
            day_sends(k, side_blocks(k)[0], 7)
            send(k, block, block, 10, partner)
        else:
            arrive(k, f_at(k, 0, 1 - x_lo), 6, home)
            block = f_at(k, 0, both)
            day_sends(k, full_blocks(k)[0], 7, home)
            send(k, block, block, 10, up_y, home)
            send(k, block, block, 10, down_y, home, extra=5)

    def beside_days(k):
        day_forwards(k, *near_blocks(k), 2, other_chip)
        if KINDS[k] == "A":
            day_forwards(k, *side_blocks(k), 7)
        else:
            day_forwards(k, *full_blocks(k), 7, home)

    def later_days(k):
        day_arrivals(k, near_blocks(k)[1], 2, other_chip)
        block = n_at(k, later, mine)
        send(k, block, block, 5, sibling, other_chip)
        if KINDS[k] == "A":
            day_arrivals(k, side_blocks(k)[1], 7)
            block = f_at(k, later, x_lo)
            send(k, block, block, 11, partner)
        else:
            day_arrivals(k, full_blocks(k)[1], 7, home)
            if KINDS[k] == "B":
                block = f_at(k, later, both)
                send(k, block, block, 11, up_y, home)
                send(k, block, block, 11, down_y, home, extra=5)
        block, place = f_at(k, later, x_lo), n_at(k, later)
        send(k, block, place, 5, sibling, home)
        act(home, lambda: pltpu.make_async_copy(block, place, here.at[k, 0]).start())

    def relay_own(k):
        if KINDS[k] != "A":
            relay(k, f_at(k, 0, both), 10)
        if KINDS[k] == "M":
            day_sends(k, full_blocks(k)[0], 7, beside)

    def relay_later(k):
        if KINDS[k] == "B":
            relay(k, f_at(k, later, both), 11)
        if KINDS[k] == "M":
            arrive(k, f_at(k, 0, both), 10, far)
            day_sends(k, full_blocks(k)[0], 7, far)

    def last_days(k):
        if KINDS[k] == "M":
            day_forwards(k, *full_blocks(k), 7, away)

    def relay(k, block, slot):
        arrive(k, block, slot, beside)
        send(k, block, block, slot, up_y, relay_up)
        send(k, block, block, slot, down_y, relay_down)

    def finish(k):
        arrive(k, n_at(k, later, theirs), 5, other_chip)
        arrive(k, n_at(k, later), 5, home_sibling)
        act(home, lambda: pltpu.make_async_copy(f_at(k, later, x_lo), n_at(k, later), here.at[k, 0]).wait())
        if KINDS[k] == "A":
            arrive(k, f_at(k, 0, 1 - x_lo), 10)
            arrive(k, f_at(k, later, 1 - x_lo), 11)
        elif KINDS[k] == "B":
            arrive(k, f_at(k, 0, both), 10, far)
            arrive(k, f_at(k, later, both), 11, far)
        else:
            day_arrivals(k, full_blocks(k)[1], 7, away)

    lane = lax.broadcasted_iota(jnp.int32, (64, 2 * WIDE), 1)
    real = (lane // 16) % 2 == 0
    place = (lax.broadcasted_iota(jnp.int32, (1, 2 * WIDE), 1) // 32) % PACK
    masks = [jnp.where(place == at, 1.0, 0.0).astype(jnp.bfloat16) for at in range(PACK)]

    def columns(d, slot):
        return jnp.concatenate([near[d, slot, v] for v in ORDER], axis=0)

    def rows(d, slot):
        return jnp.concatenate([full[d, slot, side, v] for side in range(2) for v in ORDER], axis=0)

    def pair_counts():
        total = jnp.zeros((64, WIDE), jnp.float32)
        for d in range(DAYS):
            total += lax.dot_general(columns(d, 0), rows(d, 0), NT, preferred_element_type=jnp.float32)
        inverse[...] = 1.0 / jnp.maximum(total, 1.0)

    def stack_group(group):
        slot = group + 1
        total = None
        for pair in range(DAYS // 2):
            col = jnp.concatenate([columns(2 * pair, slot), columns(2 * pair + 1, slot)], axis=1)
            row = jnp.concatenate([rows(2 * pair, slot), rows(2 * pair + 1, slot)], axis=1)
            wide = col.astype(jnp.float32)
            swapped = jnp.where(real, -pltpu.roll(wide, 2 * WIDE - 16, 1), pltpu.roll(wide, 16, 1))
            swapped = swapped.astype(jnp.bfloat16)
            left = jnp.concatenate([side * mask for mask in masks for side in (col, swapped)], axis=0)
            term = lax.dot_general(left, row, NT, preferred_element_type=jnp.float32)
            total = term if total is None else total + term
        total = total.reshape(8, 64, WIDE)
        start = group * 8
        for at in range(0, 64, 8):
            stack[at : at + 8, pl.ds(start, 8), :] = swap8(total[:, at : at + 8, :])

    def split_table():
        table_copy.wait()
        high = exact[...].astype(jnp.bfloat16)
        table[:WIDE] = high
        table[WIDE:] = (exact[...] - high.astype(jnp.float32)).astype(jnp.bfloat16)

    def half_lags(j, half):
        span = pl.ds(half * F, F)
        values = jnp.concatenate([stack[j, span, :], stack[j + 1, span, :]], axis=1)
        high = values.astype(jnp.bfloat16)
        low = (values - high.astype(jnp.float32)).astype(jnp.bfloat16)
        first = jnp.dot(table[:, span], high, preferred_element_type=jnp.float32)
        second = jnp.dot(table[:WIDE, span], low, preferred_element_type=jnp.float32)
        total = first[:WIDE] + first[WIDE:] + second
        return total[:, :WIDE], total[:, WIDE:]

    def first_half(group):
        for at in range(0, 8, 2):
            j = group * 8 + at
            lags[j], lags[j + 1] = half_lags(j, 0)

    def second_half(group):
        for at in range(0, 8, 2):
            j = group * 8 + at
            for k, half in enumerate(half_lags(j, 1)):
                lags[j + k] = (lags[j + k] + half) * inverse[pl.ds(j + k, 1), :]

    def repeat(body, first, times):
        def step(at, _):
            body(at)
            return 0

        lax.fori_loop(first, first + times, step, 0)

    work = []

    def ready(k):
        if k == 0:
            work.append(pair_counts)
        first, last = max(sum(SIZES[:k]) - 1, 0), sum(SIZES[: k + 1]) - 1
        work.append(lambda: [stack_group(at) for at in range(first, last)])
        if last == GROUPS // 2:
            work.append(split_table)
            for at in range(0, 8, 2):
                work.append(lambda first=at: repeat(first_half, first, 2))

    clean_unit()
    pl.semaphore_wait(barrier, 8)
    for k in range(count):
        start_units(k)
    stages = [spread_units]
    order = (first_spread, own_day, beside_days, later_days, relay_own, relay_later, last_days, finish)
    for idle, stage in zip(IDLE, order):
        stages += [None] * idle + [stage]
    for step in range(count + len(stages) - 1):
        for at in range(len(stages)):
            if stages[at] and 0 <= step - at < count:
                stages[at](step - at)
                if work:
                    work.pop(0)()
        done = step + 1 - len(stages)
        if 0 <= done < count:
            ready(done)
        if 0 < done < count:
            sent_all(done - 1)
    for item in work:
        item()
    repeat(second_half, 0, 8)
    sent_all(count - 1)


def correlate(groups, validity, tables):
    count = len(SIZES)
    channels = groups.shape[1]
    vmem, anywhere = pl.BlockSpec(memory_space=pltpu.VMEM), pl.BlockSpec(memory_space=pl.ANY)
    return pl.pallas_call(
        correlate_kernel,
        out_shape=pltpu.VMEM((64, WIDE, WIDE), jnp.float32),
        in_specs=[vmem, anywhere, anywhere],
        out_specs=vmem,
        scratch_shapes=[
            pltpu.VMEM((DAYS, SLOTS, 4, channels, WIDE), groups.dtype),
            pltpu.VMEM((DAYS, SLOTS, 2, 4, channels, WIDE), groups.dtype),
            pltpu.VMEM((64, 2 * F, WIDE), jnp.float32),
            pltpu.VMEM((WIDE, 2 * F), jnp.float32),
            pltpu.VMEM((2 * WIDE, 2 * F), jnp.bfloat16),
            pltpu.VMEM((64, WIDE), jnp.float32),
            pltpu.VMEM(validity.shape, validity.dtype),
            pltpu.SemaphoreType.DMA((count, 14)),
            pltpu.SemaphoreType.DMA((count, 17)),
            pltpu.SemaphoreType.DMA((count, 2)),
            pltpu.SemaphoreType.DMA((2,)),
        ],
        compiler_params=pltpu.CompilerParams(collective_id=0, has_side_effects=True, vmem_limit_bytes=58 << 20),
        name="correlate",
    )(groups, validity, tables)


def arrange_kernel(lags, out):
    group = pl.program_id(0)
    turned = [lags[group * 8 + at].T for at in range(8)]
    for at in range(0, WIDE, 8):
        out[at : at + 8] = swap8(jnp.stack([tile[at : at + 8] for tile in turned]))


def arrange(lags):
    return pl.pallas_call(
        arrange_kernel,
        grid=(8,),
        out_shape=jax.ShapeDtypeStruct((WIDE, 64, WIDE), jnp.float32),
        in_specs=[pl.BlockSpec(memory_space=pltpu.VMEM)],
        out_specs=pl.BlockSpec((WIDE, 8, WIDE), lambda group: (0, group, 0)),
        compiler_params=pltpu.CompilerParams(vmem_limit_bytes=16 << 20),
        name="arrange",
    )(pltpu.with_memory_space_constraint(lags, pltpu.VMEM))


def per_device(spectra, validity):
    lags = correlate(pltpu.with_memory_space_constraint(pack_groups(spectra), pltpu.VMEM), validity, jnp.asarray(lag_tables()))
    return arrange(lags)


def solution(mesh):
    placed = (P("day", None, ("col", "row"), None), P("day", ("col", "row")))
    return jax.shard_map(
        per_device, mesh=mesh, in_specs=placed, out_specs=P("row", "col", "day"), check_vma=False
    )
```

```python
import math

import jax
import jax.numpy as jnp
import numpy as np
from jax import lax
from jax.experimental import pallas as pl
from jax.experimental.pallas import tpu as pltpu
from jax.sharding import PartitionSpec as P

F = 256
LAGS = 512
ROWS, COLS, DAYS = 4, 8, 4
PACK = 4
GROUPS = F // PACK
SLOTS = GROUPS + 1
WIDE = 128
CHUNKS = "B4 A4 M4 B4 A4 M4 B4 A5 B4 A4 M4 B4 A4 B4 A4 A4"
KINDS = [name[0] for name in CHUNKS.split()]
SIZES = [int(name[1:]) for name in CHUNKS.split()]
IDLE = (1, 1, 1, 1, 1, 0, 1, 1)
ORDER = (0, 2, 1, 3)
MESH = pl.DeviceIdType.MESH
NT = (((1,), (1,)), ((), ()))


def lag_tables():
    lag = np.arange(LAGS) - LAGS // 2
    freq = np.arange(F)
    phase = 2.0 * math.pi / (2 * F) * np.mod(lag[:, None] * freq[None, :], 2 * F)
    both = np.stack([np.cos(phase), -np.sin(phase)]) / math.sqrt(F)
    both = both.reshape(2, DAYS, LAGS // DAYS, PACK, GROUPS).transpose(1, 2, 4, 3, 0)
    return both.reshape(DAYS, LAGS // DAYS, 2 * F).astype(np.float32)


def pack_groups(spectra):
    windows, _, channels, _ = spectra.shape
    split = jnp.transpose(spectra, (3, 2, 1, 0)).reshape(PACK, GROUPS, channels, 2 * windows)
    return jnp.transpose(split, (1, 2, 0, 3)).reshape(GROUPS, channels, WIDE)


def swap8(block):
    return jnp.swapaxes(block, 0, 1)


def correlate_kernel(
    groups, validity, tables, lags, near, full, stack, exact, table, inverse, usable, recv, sent, here, fetch
):
    row, col, day = lax.axis_index("row"), lax.axis_index("col"), lax.axis_index("day")
    core, x_hi, x_lo, y = row % 2, row // 2, col % 2, col // 2
    sibling = {"row": row + 1 - 2 * core}
    opposite = {"row": (row + 2) % ROWS}
    partner = {"col": col + 1 - 2 * x_lo}
    up_y, down_y = {"col": (col + 2) % COLS}, {"col": (col + COLS - 2) % COLS}
    days = [{"day": (day + step) % DAYS} for step in range(DAYS)]
    offset = (y + 4 - row) % 4
    home = offset == 0
    away = offset != 0
    beside = jnp.logical_or(offset == 1, offset == 3)
    far = offset == 2
    relay_up = jnp.logical_and(core == 1, offset == 1)
    relay_down = jnp.logical_and(core == 0, offset == 3)
    home_chip = x_hi == y // 2
    other_chip = x_hi != y // 2
    home_sibling = jnp.logical_and(home_chip, away)

    barrier = pltpu.get_barrier_semaphore()
    for peer in (sibling, opposite, partner, up_y, down_y, *days[1:]):
        pl.semaphore_signal(barrier, inc=1, device_id=peer, device_id_type=MESH)

    flag_copy = pltpu.make_async_copy(validity, usable, fetch.at[0])
    flag_copy.start()
    table_copy = pltpu.make_async_copy(tables.at[day], exact, fetch.at[1])
    table_copy.start()

    count = len(SIZES)
    spans = [pl.ds(sum(SIZES[:k]), SIZES[k]) for k in range(count)]
    mine, theirs = pl.ds(2 * core, 2), pl.ds(2 - 2 * core, 2)
    my_unit = 2 * core + x_hi
    all_units, both, later = pl.ds(0, 4), pl.ds(0, 2), pl.ds(1, DAYS - 1)
    pending = [[] for _ in range(count)]

    def act(when, body):
        if when is None:
            body()
        else:
            pl.when(when)(body)

    def send(k, src, dst, slot, peer, when=None, extra=0):
        def make():
            return pltpu.make_async_remote_copy(
                src_ref=src, dst_ref=dst, send_sem=sent.at[k, slot + extra], recv_sem=recv.at[k, slot],
                device_id=peer, device_id_type=MESH)

        act(when, lambda: make().start())
        pending[k].append((make, when))

    def arrive(k, dst, slot, when=None):
        act(when, lambda: pltpu.make_async_copy(dst, dst, recv.at[k, slot]).wait())

    def sent_all(k):
        for make, when in pending[k]:
            act(when, lambda make=make: make().wait_send())

    def n_at(k, d, part=all_units):
        return near.at[d, spans[k], part]

    def f_at(k, d, side, part=all_units):
        return full.at[d, spans[k], side, part]

    def day_sends(k, place, slot, when=None):
        send(k, place(0), place(DAYS - 1), slot, days[1], when)
        send(k, place(0), place(1), slot + 2, days[DAYS - 1], when)

    def day_forwards(k, place, half, slot, when=None):
        arrive(k, place(DAYS - 1), slot, when)
        send(k, half(DAYS - 1, 0), half(2, 0), slot + 1, days[1], when)
        arrive(k, place(1), slot + 2, when)
        send(k, half(1, 1), half(2, 1), 12 if slot == 2 else 13, days[DAYS - 1], when)

    def day_arrivals(k, half, slot, when=None):
        arrive(k, half(2, 0), slot + 1, when)
        arrive(k, half(2, 1), 12 if slot == 2 else 13, when)

    def near_blocks(k):
        return lambda d: n_at(k, d, mine), lambda d, part: n_at(k, d, pl.ds(2 * core + part, 1))

    def side_blocks(k):
        return lambda d: f_at(k, d, x_lo), lambda d, part: f_at(k, d, x_lo, pl.ds(2 * part, 2))

    def full_blocks(k):
        return lambda d: f_at(k, d, both), lambda d, part: f_at(k, d, part)

    def clean_unit():
        windows, channels = usable.shape
        flag_copy.wait()
        lanes = lax.broadcasted_iota(jnp.int32, (windows, WIDE), 1) % windows
        spread = (lanes == lax.broadcasted_iota(jnp.int32, (windows, WIDE), 0)).astype(jnp.bfloat16)
        flags = usable[...].astype(jnp.float32).astype(jnp.bfloat16)
        flags = lax.dot_general(flags, spread, (((0,), (0,)), ((), ())), preferred_element_type=jnp.float32)
        first = lax.broadcasted_iota(jnp.int32, (channels, WIDE), 1) < windows
        near[0, 0, my_unit] = jnp.where(first, flags, 0.0).astype(jnp.bfloat16)
        flags = flags.astype(jnp.bfloat16)
        for at in range(GROUPS):
            near[0, at + 1, my_unit] = groups[at] * flags

    def start_units(k):
        place = near.at[0, spans[k], my_unit]
        send(k, place, place, 0, opposite)

    def spread_units(k):
        arrive(k, near.at[0, spans[k], 2 * core + 1 - x_hi], 0)
        block = n_at(k, 0, mine)
        send(k, block, block, 1, sibling)
        day_sends(k, near_blocks(k)[0], 2, other_chip)

    def first_spread(k):
        arrive(k, n_at(k, 0, theirs), 1)
        block, place = n_at(k, 0), f_at(k, 0, x_lo)

        @pl.when(home)
        def _():
            copy = pltpu.make_async_copy(block, place, here.at[k, 1])
            copy.start()
            copy.wait()

        if KINDS[k] == "A":
            send(k, block, place, 6, up_y, home)
            send(k, block, place, 6, down_y, home, extra=8)
        else:
            send(k, block, place, 6, partner, home)

    def own_day(k):
        if KINDS[k] == "A":
            block = f_at(k, 0, x_lo)
            arrive(k, block, 6, away)
            send(k, block, block, 6, up_y, relay_up)
            send(k, block, block, 6, down_y, relay_down)
            day_sends(k, side_blocks(k)[0], 7)
            send(k, block, block, 10, partner)
        else:
            arrive(k, f_at(k, 0, 1 - x_lo), 6, home)
            block = f_at(k, 0, both)
            day_sends(k, full_blocks(k)[0], 7, home)
            send(k, block, block, 10, up_y, home)
            send(k, block, block, 10, down_y, home, extra=5)

    def beside_days(k):
        day_forwards(k, *near_blocks(k), 2, other_chip)
        if KINDS[k] == "A":
            day_forwards(k, *side_blocks(k), 7)
        else:
            day_forwards(k, *full_blocks(k), 7, home)

    def later_days(k):
        day_arrivals(k, near_blocks(k)[1], 2, other_chip)
        block = n_at(k, later, mine)
        send(k, block, block, 5, sibling, other_chip)
        if KINDS[k] == "A":
            day_arrivals(k, side_blocks(k)[1], 7)
            block = f_at(k, later, x_lo)
            send(k, block, block, 11, partner)
        else:
            day_arrivals(k, full_blocks(k)[1], 7, home)
            if KINDS[k] == "B":
                block = f_at(k, later, both)
                send(k, block, block, 11, up_y, home)
                send(k, block, block, 11, down_y, home, extra=5)
        block, place = f_at(k, later, x_lo), n_at(k, later)
        send(k, block, place, 5, sibling, home)
        act(home, lambda: pltpu.make_async_copy(block, place, here.at[k, 0]).start())

    def relay_own(k):
        if KINDS[k] != "A":
            relay(k, f_at(k, 0, both), 10)
        if KINDS[k] == "M":
            day_sends(k, full_blocks(k)[0], 7, beside)

    def relay_later(k):
        if KINDS[k] == "B":
            relay(k, f_at(k, later, both), 11)
        if KINDS[k] == "M":
            arrive(k, f_at(k, 0, both), 10, far)
            day_sends(k, full_blocks(k)[0], 7, far)

    def last_days(k):
        if KINDS[k] == "M":
            day_forwards(k, *full_blocks(k), 7, away)

    def relay(k, block, slot):
        arrive(k, block, slot, beside)
        send(k, block, block, slot, up_y, relay_up)
        send(k, block, block, slot, down_y, relay_down)

    def finish(k):
        arrive(k, n_at(k, later, theirs), 5, other_chip)
        arrive(k, n_at(k, later), 5, home_sibling)
        act(home, lambda: pltpu.make_async_copy(f_at(k, later, x_lo), n_at(k, later), here.at[k, 0]).wait())
        if KINDS[k] == "A":
            arrive(k, f_at(k, 0, 1 - x_lo), 10)
            arrive(k, f_at(k, later, 1 - x_lo), 11)
        elif KINDS[k] == "B":
            arrive(k, f_at(k, 0, both), 10, far)
            arrive(k, f_at(k, later, both), 11, far)
        else:
            day_arrivals(k, full_blocks(k)[1], 7, away)

    lane = lax.broadcasted_iota(jnp.int32, (64, 2 * WIDE), 1)
    real = (lane // 16) % 2 == 0
    place = (lax.broadcasted_iota(jnp.int32, (1, 2 * WIDE), 1) // 32) % PACK
    masks = [jnp.where(place == at, 1.0, 0.0).astype(jnp.bfloat16) for at in range(PACK)]

    def columns(d, slot):
        return jnp.concatenate([near[d, slot, v] for v in ORDER], axis=0)

    def rows(d, slot):
        return jnp.concatenate([full[d, slot, side, v] for side in range(2) for v in ORDER], axis=0)

    def pair_counts():
        total = jnp.zeros((64, WIDE), jnp.float32)
        for d in range(DAYS):
            total += lax.dot_general(columns(d, 0), rows(d, 0), NT, preferred_element_type=jnp.float32)
        inverse[...] = 1.0 / jnp.maximum(total, 1.0)

    def stack_group(group):
        slot = group + 1
        total = None
        for pair in range(DAYS // 2):
            col = jnp.concatenate([columns(2 * pair, slot), columns(2 * pair + 1, slot)], axis=1)
            row = jnp.concatenate([rows(2 * pair, slot), rows(2 * pair + 1, slot)], axis=1)
            wide = col.astype(jnp.float32)
            swapped = jnp.where(real, -pltpu.roll(wide, 2 * WIDE - 16, 1), pltpu.roll(wide, 16, 1))
            swapped = swapped.astype(jnp.bfloat16)
            left = jnp.concatenate([side * mask for mask in masks for side in (col, swapped)], axis=0)
            term = lax.dot_general(left, row, NT, preferred_element_type=jnp.float32)
            total = term if total is None else total + term
        total = total.reshape(8, 64, WIDE)
        start = group * 8
        for at in range(0, 64, 8):
            stack[at : at + 8, pl.ds(start, 8), :] = swap8(total[:, at : at + 8, :])

    def split_table():
        table_copy.wait()
        high = exact[...].astype(jnp.bfloat16)
        table[:WIDE] = high
        table[WIDE:] = (exact[...] - high.astype(jnp.float32)).astype(jnp.bfloat16)

    def half_lags(j, half):
        span = pl.ds(half * F, F)
        values = jnp.concatenate([stack[j, span, :], stack[j + 1, span, :]], axis=1)
        high = values.astype(jnp.bfloat16)
        low = (values - high.astype(jnp.float32)).astype(jnp.bfloat16)
        first = jnp.dot(table[:, span], high, preferred_element_type=jnp.float32)
        second = jnp.dot(table[:WIDE, span], low, preferred_element_type=jnp.float32)
        total = first[:WIDE] + first[WIDE:] + second
        return total[:, :WIDE], total[:, WIDE:]

    def first_half(group):
        for at in range(0, 8, 2):
            j = group * 8 + at
            lags[j], lags[j + 1] = half_lags(j, 0)

    def second_half(group):
        for at in range(0, 8, 2):
            j = group * 8 + at
            for k, half in enumerate(half_lags(j, 1)):
                lags[j + k] = (lags[j + k] + half) * inverse[pl.ds(j + k, 1), :]

    def repeat(body, first, times):
        def step(at, _):
            body(at)
            return 0

        lax.fori_loop(first, first + times, step, 0)

    work = []

    def ready(k):
        if k == 0:
            work.append(pair_counts)
        first, last = max(sum(SIZES[:k]) - 1, 0), sum(SIZES[: k + 1]) - 1
        work.append(lambda: [stack_group(at) for at in range(first, last)])
        if last == GROUPS // 2:
            work.append(split_table)
            for at in range(0, 8, 2):
                work.append(lambda first=at: repeat(first_half, first, 2))

    clean_unit()
    pl.semaphore_wait(barrier, 8)
    for k in range(count):
        start_units(k)
    stages = [spread_units]
    order = (first_spread, own_day, beside_days, later_days, relay_own, relay_later, last_days, finish)
    for idle, stage in zip(IDLE, order):
        stages += [None] * idle + [stage]
    for step in range(count + len(stages) - 1):
        for at in range(len(stages)):
            if stages[at] and 0 <= step - at < count:
                stages[at](step - at)
                if work:
                    work.pop(0)()
        done = step + 1 - len(stages)
        if 0 <= done < count:
            ready(done)
        if 0 < done < count:
            sent_all(done - 1)
    for item in work:
        item()
    repeat(second_half, 0, 8)
    sent_all(count - 1)


def correlate(groups, validity, tables):
    count = len(SIZES)
    channels = groups.shape[1]
    vmem, anywhere = pl.BlockSpec(memory_space=pltpu.VMEM), pl.BlockSpec(memory_space=pl.ANY)
    return pl.pallas_call(
        correlate_kernel,
        out_shape=pltpu.VMEM((64, WIDE, WIDE), jnp.float32),
        in_specs=[vmem, anywhere, anywhere],
        out_specs=vmem,
        scratch_shapes=[
            pltpu.VMEM((DAYS, SLOTS, 4, channels, WIDE), groups.dtype),
            pltpu.VMEM((DAYS, SLOTS, 2, 4, channels, WIDE), groups.dtype),
            pltpu.VMEM((64, 2 * F, WIDE), jnp.float32),
            pltpu.VMEM((WIDE, 2 * F), jnp.float32),
            pltpu.VMEM((2 * WIDE, 2 * F), jnp.bfloat16),
            pltpu.VMEM((64, WIDE), jnp.float32),
            pltpu.VMEM(validity.shape, validity.dtype),
            pltpu.SemaphoreType.DMA((count, 14)),
            pltpu.SemaphoreType.DMA((count, 17)),
            pltpu.SemaphoreType.DMA((count, 2)),
            pltpu.SemaphoreType.DMA((2,)),
        ],
        compiler_params=pltpu.CompilerParams(collective_id=0, has_side_effects=True, vmem_limit_bytes=58 << 20),
        name="correlate",
    )(groups, validity, tables)


def arrange_kernel(lags, out):
    width = out.shape[1]
    for first in range(0, width, 8):
        start = pl.program_id(0) * width + first
        turned = [lags[start + at].T for at in range(8)]
        for at in range(0, WIDE, 8):
            out[at : at + 8, first : first + 8] = swap8(jnp.stack([tile[at : at + 8] for tile in turned]))


def arrange(lags):
    return pl.pallas_call(
        arrange_kernel,
        grid=(2,),
        out_shape=jax.ShapeDtypeStruct((WIDE, 64, WIDE), jnp.float32),
        in_specs=[pl.BlockSpec(memory_space=pltpu.VMEM)],
        out_specs=pl.BlockSpec((WIDE, 32, WIDE), lambda half: (0, half, 0)),
        compiler_params=pltpu.CompilerParams(vmem_limit_bytes=16 << 20),
        name="arrange",
    )(pltpu.with_memory_space_constraint(lags, pltpu.VMEM))


def per_device(spectra, validity):
    lags = correlate(pltpu.with_memory_space_constraint(pack_groups(spectra), pltpu.VMEM), validity, jnp.asarray(lag_tables()))
    return arrange(lags)


def solution(mesh):
    placed = (P("day", None, ("col", "row"), None), P("day", ("col", "row")))
    return jax.shard_map(
        per_device, mesh=mesh, in_specs=placed, out_specs=P("row", "col", "day"), check_vma=False
    )
```
